32 devices in a mesh: sample: 8 (over y, x, core), col: 4 (over z).
Axes of the slice: x: 2, y: 2, z: 4, core: 2. Of those that a mesh axis runs over, the one named last changes fastest.
Arguments:
- block_inputs: bfloat16 [512, 17, 17, 768], P(('sample', 'col')), may hold values from 0 to 100, as said below
- first_entry: bfloat16 [1, 1, 768, 384], replicated, may hold values from -0.3125 to 0.3125
- first_wide: bfloat16 [3, 3, 192, 320], replicated, may hold values from -0.21875 to 0.21875
- first_row: bfloat16 [1, 7, 192, 192], replicated, may hold values from -0.25 to 0.25
- first_column: bfloat16 [7, 1, 192, 192], replicated, may hold values from -0.25 to 0.25
- first_reduce: bfloat16 [3, 3, 192, 192], replicated, may hold values from -0.21875 to 0.21875
- second_entry: bfloat16 [1, 1, 1280, 1152], replicated, may hold values from -0.25 to 0.25
- second_row: bfloat16 [1, 3, 384, 384], replicated, may hold values from -0.25 to 0.25
- second_column: bfloat16 [3, 1, 384, 384], replicated, may hold values from -0.25 to 0.25
- second_deep: bfloat16 [3, 3, 448, 384], replicated, may hold values from -0.125 to 0.125
- deep_row: bfloat16 [1, 3, 384, 384], replicated, may hold values from -0.25 to 0.25
- deep_column: bfloat16 [3, 1, 384, 384], replicated, may hold values from -0.25 to 0.25
- pool_project: bfloat16 [1, 1, 1280, 192], replicated, may hold values from -0.25 to 0.25
Outputs:
- feature_mean: float32 [2048], replicated
- covariance: float32 [2048, 2048], P('sample', 'col')
The draws below stay inside these ranges and needn't reach their ends.
Inputs may be any that keep to these rules, and one draw needn't show every extreme that they name: `block_inputs`: nonnegative activations.
All inputs are finite; a program needn't handle non-finite values.
Results may differ from the reference program's by a relative error of at most 0.0003.
Values sent between devices are 32-bit elements; how exact they have to be, the bound alone decides.
A program may use at most 128 MiB of HBM per device.

```python
import math
import jax
import jax.numpy as jnp
from jax import lax

GRID = 17
IN_CH = 768
RED_CH = 192
WIDE_CH = 320
BR_CH = 384
DEEP_CH = 448
POOL_CH = 192
MID_CH = 1280
FEAT = 2048
IMAGES = 512
N_COL = 4


def draw_block_inputs(key, part):
    keys = jax.random.split(key, 5)
    index = jnp.arange(IMAGES).astype(jnp.float32)
    position = index / max(IMAGES - 1, 1)
    spread = jnp.exp(jax.random.uniform(keys[0], (IMAGES,), jnp.float32, 0.0, math.log(3.4)))
    channel = jnp.exp(jax.random.uniform(keys[1], (IN_CH,), jnp.float32, math.log(0.5), math.log(2.0)))
    shape = (IMAGES, GRID, GRID, IN_CH)
    trend = jnp.exp(position * math.log(3.0))
    values = jnp.clip(jnp.abs(jax.random.normal(keys[4], shape, jnp.float32)), 0.0, 6.0)
    scale = trend * spread * 0.25
    return (values * scale[:, None, None, None] * channel).astype(jnp.bfloat16)


def gaussian(own_key, extent, deviation, limit, kind=jnp.bfloat16):
    values = jax.random.normal(own_key, extent, jnp.float32) * deviation
    return jnp.minimum(jnp.maximum(values, -limit), limit).astype(kind)


def setup_inputs(seed: int = 0) -> dict:
    key_list = jax.random.split(jax.random.key(seed), 14)
    return {
        "block_inputs": draw_block_inputs(jax.random.fold_in(key_list[13], 71), 0),
        "first_entry": gaussian(key_list[1], (1, 1, IN_CH, 2 * RED_CH), (IN_CH // 2) ** -0.5, 0.3125),
        "first_wide": gaussian(key_list[2], (3, 3, RED_CH, WIDE_CH), (9 * RED_CH // 2) ** -0.5, 0.21875),
        "first_row": gaussian(key_list[3], (1, 7, RED_CH, RED_CH), (7 * RED_CH // 2) ** -0.5, 0.25),
        "first_column": gaussian(key_list[4], (7, 1, RED_CH, RED_CH), (7 * RED_CH // 2) ** -0.5, 0.25),
        "first_reduce": gaussian(key_list[5], (3, 3, RED_CH, RED_CH), (9 * RED_CH // 2) ** -0.5, 0.21875),
        "second_entry": gaussian(key_list[6], (1, 1, MID_CH, WIDE_CH + BR_CH + DEEP_CH), (MID_CH // 2) ** -0.5, 0.25),
        "second_row": gaussian(key_list[7], (1, 3, BR_CH, BR_CH), (3 * BR_CH // 2) ** -0.5, 0.25),
        "second_column": gaussian(key_list[8], (3, 1, BR_CH, BR_CH), (3 * BR_CH // 2) ** -0.5, 0.25),
        "second_deep": gaussian(key_list[9], (3, 3, DEEP_CH, BR_CH), (9 * DEEP_CH // 2) ** -0.5, 0.125),
        "deep_row": gaussian(key_list[10], (1, 3, BR_CH, BR_CH), (3 * BR_CH // 2) ** -0.5, 0.25),
        "deep_column": gaussian(key_list[11], (3, 1, BR_CH, BR_CH), (3 * BR_CH // 2) ** -0.5, 0.25),
        "pool_project": gaussian(key_list[12], (1, 1, MID_CH, POOL_CH), (MID_CH // 2) ** -0.5, 0.25),
    }


def rectify(inputs, kernel, stride, padding):
    result = lax.conv_general_dilated(inputs, kernel, (stride, stride), padding, dimension_numbers=("NHWC", "HWIO", "NHWC"), preferred_element_type=jnp.float32)
    return jnp.maximum(result, 0.0).astype(jnp.bfloat16)


def spatial_mean(inputs):
    return jnp.mean(inputs.astype(jnp.float32), axis=(1, 2))


def network(block_inputs, first_entry, first_wide, first_row, first_column, first_reduce, second_entry, second_row, second_column, second_deep, deep_row, deep_column, pool_project):
    no_margin = ((0, 0), (0, 0))
    entry_out = rectify(block_inputs, first_entry, 1, no_margin)
    half_width = first_wide.shape[2]
    wide_out = rectify(entry_out[..., :half_width], first_wide, 2, no_margin)
    tower_out = rectify(entry_out[..., half_width:], first_row, 1, ((0, 0), (3, 3)))
    tower_out = rectify(tower_out, first_column, 1, ((3, 3), (0, 0)))
    tower_out = rectify(tower_out, first_reduce, 2, no_margin)
    maximum = lax.reduce_window(block_inputs, jnp.array(-jnp.inf, block_inputs.dtype), lax.max, (1, 3, 3, 1), (1, 2, 2, 1), "VALID")
    middle = jnp.concatenate([wide_out, tower_out, maximum], axis=3)
    second = rectify(middle, second_entry, 1, no_margin)
    branch_width = second_row.shape[2]
    deep_width = second_deep.shape[2]
    plain_width = second_entry.shape[3] - branch_width - deep_width
    plain_out = second[..., :plain_width]
    branch_in = second[..., plain_width:plain_width + branch_width]
    deep_in = second[..., plain_width + branch_width:]
    row_a = rectify(branch_in, second_row, 1, ((0, 0), (1, 1)))
    col_a = rectify(branch_in, second_column, 1, ((1, 1), (0, 0)))
    deep_out = rectify(deep_in, second_deep, 1, ((1, 1), (1, 1)))
    row_b = rectify(deep_out, deep_row, 1, ((0, 0), (1, 1)))
    col_b = rectify(deep_out, deep_column, 1, ((1, 1), (0, 0)))
    pool_pad = ((0, 0), (1, 1), (1, 1), (0, 0))
    summed = lax.reduce_window(middle.astype(jnp.float32), jnp.array(0.0, jnp.float32), lax.add, (1, 3, 3, 1), (1, 1, 1, 1), pool_pad)
    ones_map = jnp.ones((1, middle.shape[1], middle.shape[2], 1), jnp.float32)
    cell_count = lax.reduce_window(ones_map, jnp.array(0.0, jnp.float32), lax.add, (1, 3, 3, 1), (1, 1, 1, 1), pool_pad)
    averaged = (summed / cell_count).astype(jnp.bfloat16)
    pooled = rectify(averaged, pool_project, 1, no_margin)
    return jnp.concatenate([spatial_mean(plain_out), spatial_mean(row_a), spatial_mean(col_a), spatial_mean(row_b), spatial_mean(col_b), spatial_mean(pooled)], axis=1)


def reference(block_inputs, first_entry, first_wide, first_row, first_column, first_reduce, second_entry, second_row, second_column, second_deep, deep_row, deep_column, pool_project):
    batches = block_inputs.reshape((IMAGES // N_COL, N_COL) + block_inputs.shape[1:])

    def one_batch(images):
        return network(images, first_entry, first_wide, first_row, first_column, first_reduce, second_entry, second_row, second_column, second_deep, deep_row, deep_column, pool_project)

    features = lax.map(one_batch, batches).reshape((IMAGES, FEAT))
    feature_mean = jnp.sum(features, axis=0) / IMAGES
    centered = features - feature_mean
    covariance = jnp.einsum("nf,ng->fg", centered, centered, precision=lax.Precision.HIGHEST, preferred_element_type=jnp.float32) / (IMAGES - 1)
    return (feature_mean, covariance)
```

```python
import functools

import jax
import jax.numpy as jnp
from jax import lax
from jax.experimental import pallas as pl
from jax.experimental.pallas import tpu as pltpu
from jax.sharding import PartitionSpec as P


def rectify(inputs, kernel, stride, padding):
    result = lax.conv_general_dilated(
        inputs,
        kernel,
        (stride, stride),
        padding,
        dimension_numbers=("NHWC", "HWIO", "NHWC"),
        preferred_element_type=jnp.float32,
    )
    return jnp.maximum(result, 0.0).astype(jnp.bfloat16)


def spatial_mean(inputs):
    return jnp.mean(inputs.astype(jnp.float32), axis=(1, 2))


def network(
    block_inputs,
    first_entry,
    first_wide,
    first_row,
    first_column,
    first_reduce,
    second_entry,
    second_row,
    second_column,
    second_deep,
    deep_row,
    deep_column,
    pool_project,
):
    no_margin = ((0, 0), (0, 0))
    entry_out = rectify(block_inputs, first_entry, 1, no_margin)
    half_width = first_wide.shape[2]
    wide_out = rectify(entry_out[..., :half_width], first_wide, 2, no_margin)
    tower_out = rectify(entry_out[..., half_width:], first_row, 1, ((0, 0), (3, 3)))
    tower_out = rectify(tower_out, first_column, 1, ((3, 3), (0, 0)))
    tower_out = rectify(tower_out, first_reduce, 2, no_margin)
    maximum = lax.reduce_window(
        block_inputs,
        jnp.array(-jnp.inf, block_inputs.dtype),
        lax.max,
        (1, 3, 3, 1),
        (1, 2, 2, 1),
        "VALID",
    )
    middle = jnp.concatenate([wide_out, tower_out, maximum], axis=3)
    second = rectify(middle, second_entry, 1, no_margin)
    branch_width = second_row.shape[2]
    deep_width = second_deep.shape[2]
    plain_width = second_entry.shape[3] - branch_width - deep_width
    plain_out = second[..., :plain_width]
    branch_in = second[..., plain_width : plain_width + branch_width]
    deep_in = second[..., plain_width + branch_width :]
    row_a = rectify(branch_in, second_row, 1, ((0, 0), (1, 1)))
    col_a = rectify(branch_in, second_column, 1, ((1, 1), (0, 0)))
    deep_out = rectify(deep_in, second_deep, 1, ((1, 1), (1, 1)))
    row_b = rectify(deep_out, deep_row, 1, ((0, 0), (1, 1)))
    col_b = rectify(deep_out, deep_column, 1, ((1, 1), (0, 0)))
    pool_pad = ((0, 0), (1, 1), (1, 1), (0, 0))
    summed = lax.reduce_window(
        middle.astype(jnp.float32),
        jnp.array(0.0, jnp.float32),
        lax.add,
        (1, 3, 3, 1),
        (1, 1, 1, 1),
        pool_pad,
    )
    ones_map = jnp.ones((1, middle.shape[1], middle.shape[2], 1), jnp.float32)
    cell_count = lax.reduce_window(
        ones_map, jnp.array(0.0, jnp.float32), lax.add, (1, 3, 3, 1), (1, 1, 1, 1), pool_pad
    )
    averaged = (summed / cell_count).astype(jnp.bfloat16)
    pooled = rectify(averaged, pool_project, 1, no_margin)
    return jnp.concatenate(
        [
            spatial_mean(plain_out),
            spatial_mean(row_a),
            spatial_mean(col_a),
            spatial_mean(row_b),
            spatial_mean(col_b),
            spatial_mean(pooled),
        ],
        axis=1,
    )


def exchange_kernel(
    n_sample,
    n_col,
    feats_ref,
    mean_ref,
    cov_ref,
    cols,
    rows,
    sums_col,
    sums_sample,
    col_send,
    col_recv,
    row_send,
    row_recv,
    sum_send,
    sum_recv,
    cols_send,
    cols_recv,
    rows_send,
    rows_recv,
    total_send,
    total_recv,
):
    s = lax.axis_index("sample")
    c = lax.axis_index("col")
    images = feats_ref.shape[0]
    col_width = cols.shape[3]
    row_width = rows.shape[3]
    total_images = images * n_sample * n_col
    mesh_id = pl.DeviceIdType.MESH

    def col_at(index):
        return pl.ds(pl.multiple_of(index * col_width, 128), col_width)

    def row_at(index):
        return pl.ds(pl.multiple_of(index * row_width, 128), row_width)

    def send(source, target, send_sem, recv_sem, sample, col):
        copy = pltpu.make_async_remote_copy(
            src_ref=source,
            dst_ref=target,
            send_sem=send_sem,
            recv_sem=recv_sem,
            device_id=(sample, col),
            device_id_type=mesh_id,
        )
        copy.start()
        return copy

    barrier = pltpu.get_barrier_semaphore()
    for k in range(1, n_col):
        pl.semaphore_signal(
            barrier, inc=1, device_id=(s, lax.rem(c + k, n_col)), device_id_type=mesh_id
        )
    for k in range(1, n_sample):
        pl.semaphore_signal(
            barrier, inc=1, device_id=(lax.rem(s + k, n_sample), c), device_id_type=mesh_id
        )
    sums_col[c] = jnp.sum(feats_ref[...], axis=0, keepdims=True)
    cols[s, c] = feats_ref[:, col_at(c)]
    rows[s, c] = feats_ref[:, row_at(s)]
    pl.semaphore_wait(barrier, n_col - 1 + n_sample - 1)

    sends = []
    first_cols, first_sums, first_rows = [], [], []
    for k in range(1, n_col):
        to = lax.rem(c + k, n_col)
        first_cols.append(
            send(feats_ref.at[:, col_at(to)], cols.at[s, c], col_send.at[k], col_recv.at[k], s, to)
        )
        first_sums.append(
            send(sums_col.at[c], sums_col.at[c], sum_send.at[k], sum_recv.at[k], s, to)
        )
    for k in range(1, n_sample):
        to = lax.rem(s + k, n_sample)
        first_rows.append(
            send(feats_ref.at[:, row_at(to)], rows.at[s, c], row_send.at[k], row_recv.at[k], to, c)
        )
    for copy in first_rows:
        copy.wait_recv()
    second_rows = []
    for k in range(1, n_col):
        to = lax.rem(c + k, n_col)
        second_rows.append(
            send(rows.at[:, c], rows.at[:, c], rows_send.at[k], rows_recv.at[k], s, to)
        )
    for copy in first_cols:
        copy.wait_recv()
    second_cols = []
    for k in range(1, n_sample):
        to = lax.rem(s + k, n_sample)
        second_cols.append(
            send(cols.at[s], cols.at[s], cols_send.at[k], cols_recv.at[k], to, c)
        )
    for copy in first_sums:
        copy.wait_recv()
    sums_sample[s] = jnp.sum(sums_col[...], axis=0)
    second_sums = []
    for k in range(1, n_sample):
        to = lax.rem(s + k, n_sample)
        second_sums.append(
            send(sums_sample.at[s], sums_sample.at[s], total_send.at[k], total_recv.at[k], to, c)
        )
    for copy in second_sums:
        copy.wait_recv()
    mean_ref[...] = jnp.sum(sums_sample[...], axis=0) * (1.0 / total_images)
    for copy in second_rows:
        copy.wait_recv()
    row_values = rows[...].reshape(total_images, row_width) - mean_ref[:, row_at(s)]
    row_values = row_values.T
    row_high = row_values.astype(jnp.bfloat16)
    row_low = (row_values - row_high.astype(jnp.float32)).astype(jnp.bfloat16)
    for copy in second_cols:
        copy.wait_recv()
    col_values = cols[...].reshape(total_images, col_width) - mean_ref[:, col_at(c)]
    col_high = col_values.astype(jnp.bfloat16)
    col_low = (col_values - col_high.astype(jnp.float32)).astype(jnp.bfloat16)
    product = jnp.dot(row_high, col_low, preferred_element_type=jnp.float32)
    product += jnp.dot(row_low, col_high, preferred_element_type=jnp.float32)
    product += jnp.dot(row_high, col_high, preferred_element_type=jnp.float32)
    cov_ref[...] = product * (1.0 / (total_images - 1))
    for copy in first_cols + first_sums + first_rows + second_rows + second_cols + second_sums:
        copy.wait_send()


def exchange(features):
    n_sample = lax.axis_size("sample")
    n_col = lax.axis_size("col")
    images, width = features.shape
    row_width = width // n_sample
    col_width = width // n_col
    dma = pltpu.SemaphoreType.DMA
    vmem = pl.BlockSpec(memory_space=pltpu.VMEM)
    mean, covariance = pl.pallas_call(
        functools.partial(exchange_kernel, n_sample, n_col),
        out_shape=(
            jax.ShapeDtypeStruct((1, width), jnp.float32),
            jax.ShapeDtypeStruct((row_width, col_width), jnp.float32),
        ),
        in_specs=[vmem],
        out_specs=(vmem, vmem),
        scratch_shapes=[
            pltpu.VMEM((n_sample, n_col, images, col_width), jnp.float32),
            pltpu.VMEM((n_sample, n_col, images, row_width), jnp.float32),
            pltpu.VMEM((n_col, 1, width), jnp.float32),
            pltpu.VMEM((n_sample, 1, width), jnp.float32),
            dma((n_col,)),
            dma((n_col,)),
            dma((n_sample,)),
            dma((n_sample,)),
            dma((n_col,)),
            dma((n_col,)),
            dma((n_sample,)),
            dma((n_sample,)),
            dma((n_col,)),
            dma((n_col,)),
            dma((n_sample,)),
            dma((n_sample,)),
        ],
        compiler_params=pltpu.CompilerParams(
            collective_id=0, has_side_effects=True, vmem_limit_bytes=48 * 1024 * 1024
        ),
        name="exchange",
    )(features)
    return mean.reshape(width), covariance


def local(
    block_inputs,
    first_entry,
    first_wide,
    first_row,
    first_column,
    first_reduce,
    second_entry,
    second_row,
    second_column,
    second_deep,
    deep_row,
    deep_column,
    pool_project,
):
    features = network(
        block_inputs,
        first_entry,
        first_wide,
        first_row,
        first_column,
        first_reduce,
        second_entry,
        second_row,
        second_column,
        second_deep,
        deep_row,
        deep_column,
        pool_project,
    )
    return exchange(features)


def solution(mesh):
    placed = (
        P(("sample", "col"), None, None, None),
        P(),
        P(),
        P(),
        P(),
        P(),
        P(),
        P(),
        P(),
        P(),
        P(),
        P(),
        P(),
    )
    return jax.shard_map(
        local, mesh=mesh, in_specs=placed, out_specs=(P(), P("sample", "col")), check_vma=False
    )
```

```python
import functools

import jax
import jax.numpy as jnp
from jax import lax
from jax.experimental import pallas as pl
from jax.experimental.pallas import tpu as pltpu
from jax.sharding import PartitionSpec as P


def rectified(lhs, weights):
    out = jnp.dot(lhs, weights, preferred_element_type=jnp.float32)
    return jnp.maximum(out, 0.0).astype(jnp.bfloat16)


def network_kernel(
    x_hbm,
    entry_hbm,
    wide_hbm,
    row_hbm,
    column_hbm,
    reduce_hbm,
    second_hbm,
    second_row_hbm,
    second_column_hbm,
    deep_hbm,
    deep_row_hbm,
    deep_column_hbm,
    project_hbm,
    feats_ref,
    x_buf,
    entry_w,
    wide_w,
    row_w,
    column_w,
    reduce_w,
    second_w,
    second_row_w,
    second_column_w,
    deep_w,
    deep_row_w,
    deep_column_w,
    project_w,
    short_buf,
    long_buf,
    column_buf,
    tower_buf,
    mid_buf,
    branch_buf,
    deep_buf,
    deep_out_buf,
    average_buf,
    x_sem,
    w_sem,
):
    grid, _, images, in_ch = x_buf.shape
    half = row_hbm.shape[1]
    half_pad = row_w.shape[1]
    wide = wide_hbm.shape[2]
    small = mid_buf.shape[0] - 2
    mid_ch = mid_buf.shape[3]
    branch = second_row_hbm.shape[1]
    deep_in = deep_hbm.shape[1]
    deep_pad = deep_w.shape[1]
    plain = second_hbm.shape[1] - branch - deep_in
    margin = (row_hbm.shape[0] - 1) // 2

    for ref in (wide_w, row_w, column_w, reduce_w):
        ref[:, half:] = jnp.zeros((ref.shape[0], half_pad - half, ref.shape[2]), ref.dtype)
    deep_w[:, deep_in:] = jnp.zeros(
        (deep_w.shape[0], deep_pad - deep_in, deep_w.shape[2]), deep_w.dtype
    )

    def row_copy(h):
        return pltpu.make_async_copy(x_hbm.at[h], x_buf.at[h], x_sem.at[h])

    pairs = (
        (entry_hbm, entry_w),
        (row_hbm, row_w.at[:, 0:half]),
        (column_hbm, column_w.at[:, 0:half]),
        (wide_hbm, wide_w.at[:, 0:half]),
        (reduce_hbm, reduce_w.at[:, 0:half]),
        (second_hbm, second_w),
        (second_row_hbm, second_row_w),
        (second_column_hbm, second_column_w),
        (deep_hbm, deep_w.at[:, 0:deep_in]),
        (deep_row_hbm, deep_row_w),
        (deep_column_hbm, deep_column_w),
        (project_hbm, project_w),
    )
    copies = [
        pltpu.make_async_copy(source, target, w_sem.at[i])
        for i, (source, target) in enumerate(pairs)
    ]
    copies[0].start()
    for h in range(grid):
        row_copy(h).start()
    for copy in copies[1:]:
        copy.start()

    low = half // 128 * 128
    for ref in (short_buf, column_buf, tower_buf):
        ref[..., low:] = jnp.zeros(ref.shape[:3] + (ref.shape[3] - low,), ref.dtype)
    long_buf[..., low:] = jnp.zeros(long_buf.shape[:3] + (half_pad - low,), long_buf.dtype)
    for edge in (pl.ds(0, margin), pl.ds(grid + margin, margin)):
        long_buf[:, edge] = jnp.zeros((grid, margin, images, half_pad), long_buf.dtype)
        column_buf[edge] = jnp.zeros((margin, grid, images, half_pad), column_buf.dtype)
    deep_low = deep_in // 128 * 128
    deep_buf[..., deep_low:] = jnp.zeros(
        deep_buf.shape[:3] + (deep_pad - deep_low,), deep_buf.dtype
    )
    for ref in (mid_buf, branch_buf, deep_buf, deep_out_buf):
        line = jnp.zeros((small + 2, images, ref.shape[3]), ref.dtype)
        ref[0] = line
        ref[small + 1] = line
        ref[:, 0] = line
        ref[:, small + 1] = line

    copies[0].wait()

    def entry_step(h, carry):
        row_copy(h).wait()
        out = rectified(x_buf[h].reshape(grid * images, in_ch), entry_w[...])
        short_buf[h, :, :, 0:half] = out[:, 0:half].reshape(grid, images, half)
        long_buf[h, pl.ds(margin, grid), :, 0:half] = out[:, half:].reshape(grid, images, half)
        return carry

    lax.fori_loop(0, grid, entry_step, 0)

    copies[1].wait()

    def row_step(h, carry):
        lhs = jnp.concatenate(
            [
                long_buf[h, pl.ds(j, grid)].reshape(grid * images, half_pad)
                for j in range(2 * margin + 1)
            ],
            axis=1,
        )
        out = rectified(lhs, row_w[...].reshape(-1, half))
        column_buf[h + margin, :, :, 0:half] = out.reshape(grid, images, half)
        return carry

    lax.fori_loop(0, grid, row_step, 0)

    copies[2].wait()

    def column_step(h, carry):
        lhs = jnp.concatenate(
            [
                column_buf[h + i].reshape(grid * images, half_pad)
                for i in range(2 * margin + 1)
            ],
            axis=1,
        )
        out = rectified(lhs, column_w[...].reshape(-1, half))
        tower_buf[h, :, :, 0:half] = out.reshape(grid, images, half)
        return carry

    lax.fori_loop(0, grid, column_step, 0)

    group = 4
    n_groups = small // group

    def strided(ref, r, j):
        start, odd = j // 2, (j + 1) // 2
        width = ref.shape[3]
        return ref[r, pl.ds(start, 2 * small)].reshape(small, 2, images, width)[:, odd]

    def strided_taps(ref, h):
        return jnp.concatenate(
            [
                jnp.concatenate(
                    [strided(ref, 2 * (h + g) + i, j) for g in range(group)], axis=0
                ).reshape(group * small * images, half_pad)
                for i in range(3)
                for j in range(3)
            ],
            axis=1,
        )

    copies[3].wait()
    copies[4].wait()

    def middle_step(step, carry):
        h = step * group
        wide_out = rectified(strided_taps(short_buf, h), wide_w[...].reshape(-1, wide))
        tower_out = rectified(strided_taps(tower_buf, h), reduce_w[...].reshape(-1, half))
        both = jnp.concatenate([wide_out, tower_out], axis=1)
        mid_buf[pl.ds(h + 1, group), pl.ds(1, small), :, 0 : wide + half] = both.reshape(
            group, small, images, wide + half
        )
        for g in range(group):
            for lane in range(0, in_ch, 256):
                lanes = pl.ds(lane, 256)
                r = 2 * (h + g)
                tall = jnp.maximum(
                    jnp.maximum(x_buf[r, :, :, lanes], x_buf[r + 1, :, :, lanes]),
                    x_buf[r + 2, :, :, lanes],
                )
                even = tall[0 : 2 * small].reshape(small, 2, images, 256)
                late = tall[1 : 2 * small + 1].reshape(small, 2, images, 256)
                mid_buf[h + g + 1, pl.ds(1, small), :, pl.ds(wide + half + lane, 256)] = (
                    jnp.maximum(jnp.maximum(even[:, 0], even[:, 1]), late[:, 1])
                )
        return carry

    lax.fori_loop(0, n_groups, middle_step, 0)

    rows_m = group * small * images
    here = pl.ds(1, small)

    def total(out):
        width = out.shape[1]
        return jnp.sum(out.astype(jnp.float32).reshape(group * small, images, width), axis=0)

    copies[5].wait()

    def second_step(step, plain_sum):
        h = step * group
        lhs = mid_buf[pl.ds(h + 1, group), here].reshape(rows_m, mid_ch)
        out = rectified(lhs, second_w[...])
        branch_buf[pl.ds(h + 1, group), here] = out[:, plain : plain + branch].reshape(
            group, small, images, branch
        )
        deep_buf[pl.ds(h + 1, group), here, :, 0:deep_in] = out[:, plain + branch :].reshape(
            group, small, images, deep_in
        )
        return plain_sum + total(out[:, 0:plain])

    plain_sum = lax.fori_loop(
        0, n_groups, second_step, jnp.zeros((images, plain), jnp.float32)
    )

    def window(ref, h, rows, cols):
        return jnp.concatenate(
            [
                ref[pl.ds(h + i, group), pl.ds(j, small)].reshape(rows_m, ref.shape[3])
                for i in rows
                for j in cols
            ],
            axis=1,
        )

    def pair_step(source, row_weights, column_weights):
        out_ch = row_weights.shape[2]

        def step_body(step, sums):
            h = step * group
            row_out = rectified(
                window(source, h, (1,), (0, 1, 2)), row_weights[...].reshape(-1, out_ch)
            )
            column_out = rectified(
                window(source, h, (0, 1, 2), (1,)), column_weights[...].reshape(-1, out_ch)
            )
            return sums[0] + total(row_out), sums[1] + total(column_out)

        zero = jnp.zeros((images, out_ch), jnp.float32)
        return lax.fori_loop(0, n_groups, step_body, (zero, zero))

    copies[6].wait()
    copies[7].wait()
    row_a, column_a = pair_step(branch_buf, second_row_w, second_column_w)

    copies[8].wait()

    def deep_step(step, carry):
        h = step * group
        lhs = window(deep_buf, h, (0, 1, 2), (0, 1, 2))
        out = rectified(lhs, deep_w[...].reshape(9 * deep_pad, -1))
        deep_out_buf[pl.ds(h + 1, group), here] = out.reshape(
            group, small, images, out.shape[1]
        )
        return carry

    lax.fori_loop(0, n_groups, deep_step, 0)

    copies[9].wait()
    copies[10].wait()
    row_b, column_b = pair_step(deep_out_buf, deep_row_w, deep_column_w)

    def average_step(chunk, carry):
        lanes = pl.ds(pl.multiple_of(chunk * 128, 128), 128)
        across = []
        for r in range(small + 2):
            line = mid_buf[r, :, :, lanes].astype(jnp.float32)
            across.append(line[0:small] + line[1 : small + 1] + line[2 : small + 2])
        for h in range(small):
            tall = 2 if h in (0, small - 1) else 3
            summed = across[h] + across[h + 1] + across[h + 2]
            average_buf[h, 0, :, lanes] = (summed[0] * (1.0 / (2 * tall))).astype(jnp.bfloat16)
            average_buf[h, pl.ds(1, small - 2), :, lanes] = (
                summed[1 : small - 1] * (1.0 / (3 * tall))
            ).astype(jnp.bfloat16)
            average_buf[h, small - 1, :, lanes] = (
                summed[small - 1] * (1.0 / (2 * tall))
            ).astype(jnp.bfloat16)
        return carry

    lax.fori_loop(0, mid_ch // 128, average_step, 0)

    copies[11].wait()

    def project_step(step, pooled_sum):
        lhs = average_buf[pl.ds(step * group, group)].reshape(rows_m, mid_ch)
        out = lax.dot_general(
            lhs, project_w[...], (((1,), (1,)), ((), ())), preferred_element_type=jnp.float32
        )
        return pooled_sum + total(jnp.maximum(out, 0.0).astype(jnp.bfloat16))

    pooled = lax.fori_loop(
        0, n_groups, project_step, jnp.zeros((images, project_w.shape[0]), jnp.float32)
    )
    features = jnp.concatenate([plain_sum, row_a, column_a, row_b, column_b, pooled], axis=1)
    feats_ref[...] = features * (1.0 / (small * small))


def network(
    block_inputs,
    first_entry,
    first_wide,
    first_row,
    first_column,
    first_reduce,
    second_entry,
    second_row,
    second_column,
    second_deep,
    deep_row,
    deep_column,
    pool_project,
):
    def flat(kernel):
        return kernel.reshape((-1,) + kernel.shape[2:])

    x = jnp.transpose(block_inputs, (1, 2, 0, 3))
    grid, _, images, in_ch = x.shape
    small = (grid - 3) // 2 + 1
    half = first_row.shape[2]
    half_pad = -(-half // 256) * 256
    deep_in = second_deep.shape[2]
    deep_pad = -(-deep_in // 128) * 128
    margin = (first_row.shape[1] - 1) // 2
    mid_ch = second_entry.shape[2]
    branch = second_row.shape[2]
    deep_ch = second_deep.shape[3]
    operands = [
        x,
        first_entry[0, 0],
        flat(first_wide),
        flat(first_row),
        flat(first_column),
        flat(first_reduce),
        second_entry[0, 0],
        flat(second_row),
        flat(second_column),
        flat(second_deep),
        flat(deep_row),
        flat(deep_column),
        pool_project[0, 0].T,
    ]
    width = second_entry.shape[3] - branch - deep_in + 2 * branch + 2 * deep_ch
    width += pool_project.shape[3]

    def scratch(*shape):
        return pltpu.VMEM(shape, jnp.bfloat16)

    def weight_scratch(kernel, depth):
        return scratch(kernel.shape[0], depth, kernel.shape[2])

    edge = small + 2
    return pl.pallas_call(
        network_kernel,
        out_shape=jax.ShapeDtypeStruct((images, width), jnp.float32),
        in_specs=[pl.BlockSpec(memory_space=pl.ANY)] * len(operands),
        out_specs=pl.BlockSpec(memory_space=pltpu.VMEM),
        scratch_shapes=[
            scratch(*x.shape),
            scratch(*operands[1].shape),
            weight_scratch(operands[2], half_pad),
            weight_scratch(operands[3], half_pad),
            weight_scratch(operands[4], half_pad),
            weight_scratch(operands[5], half_pad),
            scratch(*operands[6].shape),
            scratch(*operands[7].shape),
            scratch(*operands[8].shape),
            weight_scratch(operands[9], deep_pad),
            scratch(*operands[10].shape),
            scratch(*operands[11].shape),
            scratch(*operands[12].shape),
            scratch(grid, grid, images, half_pad),
            scratch(grid, grid + 2 * margin, images, half_pad),
            scratch(grid + 2 * margin, grid, images, half_pad),
            scratch(grid, grid, images, half_pad),
            scratch(edge, edge, images, mid_ch),
            scratch(edge, edge, images, branch),
            scratch(edge, edge, images, deep_pad),
            scratch(edge, edge, images, deep_ch),
            scratch(small, small, images, mid_ch),
            pltpu.SemaphoreType.DMA((grid,)),
            pltpu.SemaphoreType.DMA((len(operands) - 1,)),
        ],
        compiler_params=pltpu.CompilerParams(vmem_limit_bytes=60 * 1024 * 1024),
        name="network",
    )(*operands)


def exchange_kernel(
    n_sample,
    n_col,
    feats_ref,
    mean_ref,
    cov_ref,
    cols,
    rows,
    sums_col,
    sums_sample,
    col_send,
    col_recv,
    row_send,
    row_recv,
    sum_send,
    sum_recv,
    cols_send,
    cols_recv,
    rows_send,
    rows_recv,
    total_send,
    total_recv,
):
    s = lax.axis_index("sample")
    c = lax.axis_index("col")
    images = feats_ref.shape[0]
    col_width = cols.shape[3]
    row_width = rows.shape[3]
    total_images = images * n_sample * n_col
    mesh_id = pl.DeviceIdType.MESH

    def col_at(index):
        return pl.ds(pl.multiple_of(index * col_width, 128), col_width)

    def row_at(index):
        return pl.ds(pl.multiple_of(index * row_width, 128), row_width)

    def send(source, target, send_sem, recv_sem, sample, col):
        copy = pltpu.make_async_remote_copy(
            src_ref=source,
            dst_ref=target,
            send_sem=send_sem,
            recv_sem=recv_sem,
            device_id=(sample, col),
            device_id_type=mesh_id,
        )
        copy.start()
        return copy

    barrier = pltpu.get_barrier_semaphore()
    for k in range(1, n_col):
        pl.semaphore_signal(
            barrier, inc=1, device_id=(s, lax.rem(c + k, n_col)), device_id_type=mesh_id
        )
    for k in range(1, n_sample):
        pl.semaphore_signal(
            barrier, inc=1, device_id=(lax.rem(s + k, n_sample), c), device_id_type=mesh_id
        )
    sums_col[c] = jnp.sum(feats_ref[...], axis=0, keepdims=True)
    cols[s, c] = feats_ref[:, col_at(c)]
    rows[s, c] = feats_ref[:, row_at(s)]
    pl.semaphore_wait(barrier, n_col - 1 + n_sample - 1)

    sends = []
    first_cols, first_sums, first_rows = [], [], []
    for k in range(1, n_col):
        to = lax.rem(c + k, n_col)
        first_cols.append(
            send(feats_ref.at[:, col_at(to)], cols.at[s, c], col_send.at[k], col_recv.at[k], s, to)
        )
        first_sums.append(
            send(sums_col.at[c], sums_col.at[c], sum_send.at[k], sum_recv.at[k], s, to)
        )
    for k in range(1, n_sample):
        to = lax.rem(s + k, n_sample)
        first_rows.append(
            send(feats_ref.at[:, row_at(to)], rows.at[s, c], row_send.at[k], row_recv.at[k], to, c)
        )
    for copy in first_rows:
        copy.wait_recv()
    second_rows = []
    for k in range(1, n_col):
        to = lax.rem(c + k, n_col)
        second_rows.append(
            send(rows.at[:, c], rows.at[:, c], rows_send.at[k], rows_recv.at[k], s, to)
        )
    for copy in first_cols:
        copy.wait_recv()
    second_cols = []
    for k in range(1, n_sample):
        to = lax.rem(s + k, n_sample)
        second_cols.append(
            send(cols.at[s], cols.at[s], cols_send.at[k], cols_recv.at[k], to, c)
        )
    for copy in first_sums:
        copy.wait_recv()
    sums_sample[s] = jnp.sum(sums_col[...], axis=0)
    second_sums = []
    for k in range(1, n_sample):
        to = lax.rem(s + k, n_sample)
        second_sums.append(
            send(sums_sample.at[s], sums_sample.at[s], total_send.at[k], total_recv.at[k], to, c)
        )
    for copy in second_sums:
        copy.wait_recv()
    mean_ref[...] = jnp.sum(sums_sample[...], axis=0) * (1.0 / total_images)
    for copy in second_rows:
        copy.wait_recv()
    row_values = rows[...].reshape(total_images, row_width) - mean_ref[:, row_at(s)]
    row_values = row_values.T
    row_high = row_values.astype(jnp.bfloat16)
    row_low = (row_values - row_high.astype(jnp.float32)).astype(jnp.bfloat16)
    for copy in second_cols:
        copy.wait_recv()
    col_values = cols[...].reshape(total_images, col_width) - mean_ref[:, col_at(c)]
    col_high = col_values.astype(jnp.bfloat16)
    col_low = (col_values - col_high.astype(jnp.float32)).astype(jnp.bfloat16)
    product = jnp.dot(row_high, col_low, preferred_element_type=jnp.float32)
    product += jnp.dot(row_low, col_high, preferred_element_type=jnp.float32)
    product += jnp.dot(row_high, col_high, preferred_element_type=jnp.float32)
    cov_ref[...] = product * (1.0 / (total_images - 1))
    for copy in first_cols + first_sums + first_rows + second_rows + second_cols + second_sums:
        copy.wait_send()


def exchange(features):
    n_sample = lax.axis_size("sample")
    n_col = lax.axis_size("col")
    images, width = features.shape
    row_width = width // n_sample
    col_width = width // n_col
    dma = pltpu.SemaphoreType.DMA
    vmem = pl.BlockSpec(memory_space=pltpu.VMEM)
    mean, covariance = pl.pallas_call(
        functools.partial(exchange_kernel, n_sample, n_col),
        out_shape=(
            jax.ShapeDtypeStruct((1, width), jnp.float32),
            jax.ShapeDtypeStruct((row_width, col_width), jnp.float32),
        ),
        in_specs=[vmem],
        out_specs=(vmem, vmem),
        scratch_shapes=[
            pltpu.VMEM((n_sample, n_col, images, col_width), jnp.float32),
            pltpu.VMEM((n_sample, n_col, images, row_width), jnp.float32),
            pltpu.VMEM((n_col, 1, width), jnp.float32),
            pltpu.VMEM((n_sample, 1, width), jnp.float32),
            dma((n_col,)),
            dma((n_col,)),
            dma((n_sample,)),
            dma((n_sample,)),
            dma((n_col,)),
            dma((n_col,)),
            dma((n_sample,)),
            dma((n_sample,)),
            dma((n_col,)),
            dma((n_col,)),
            dma((n_sample,)),
            dma((n_sample,)),
        ],
        compiler_params=pltpu.CompilerParams(
            collective_id=0, has_side_effects=True, vmem_limit_bytes=48 * 1024 * 1024
        ),
        name="exchange",
    )(features)
    return mean.reshape(width), covariance


def local(
    block_inputs,
    first_entry,
    first_wide,
    first_row,
    first_column,
    first_reduce,
    second_entry,
    second_row,
    second_column,
    second_deep,
    deep_row,
    deep_column,
    pool_project,
):
    features = network(
        block_inputs,
        first_entry,
        first_wide,
        first_row,
        first_column,
        first_reduce,
        second_entry,
        second_row,
        second_column,
        second_deep,
        deep_row,
        deep_column,
        pool_project,
    )
    return exchange(features)


def solution(mesh):
    placed = (
        P(("sample", "col"), None, None, None),
        P(),
        P(),
        P(),
        P(),
        P(),
        P(),
        P(),
        P(),
        P(),
        P(),
        P(),
        P(),
    )
    return jax.shard_map(
        local, mesh=mesh, in_specs=placed, out_specs=(P(), P("sample", "col")), check_vma=False
    )
```

```python
import functools

import jax
import jax.numpy as jnp
from jax import lax
from jax.experimental import pallas as pl
from jax.experimental.pallas import tpu as pltpu
from jax.sharding import PartitionSpec as P


def rectified(lhs, weights):
    out = jnp.dot(lhs, weights, preferred_element_type=jnp.float32)
    return jnp.maximum(out, 0.0).astype(jnp.bfloat16)


def network_kernel(
    x_hbm,
    entry_hbm,
    wide_hbm,
    row_hbm,
    column_hbm,
    reduce_hbm,
    second_hbm,
    second_row_hbm,
    second_column_hbm,
    deep_hbm,
    deep_row_hbm,
    deep_column_hbm,
    project_hbm,
    feats_ref,
    x_buf,
    entry_w,
    wide_w,
    row_w,
    column_w,
    reduce_w,
    second_w,
    second_row_w,
    second_column_w,
    deep_w,
    deep_row_w,
    deep_column_w,
    project_w,
    short_buf,
    long_buf,
    column_buf,
    tower_buf,
    mid_buf,
    branch_buf,
    deep_buf,
    deep_out_buf,
    average_buf,
    x_sem,
    w_sem,
):
    grid, _, images, in_ch = x_buf.shape
    half = row_hbm.shape[1]
    half_pad = row_w.shape[1]
    wide = wide_hbm.shape[2]
    small = mid_buf.shape[0] - 2
    mid_ch = mid_buf.shape[3]
    branch = second_row_hbm.shape[1]
    deep_in = deep_hbm.shape[1]
    deep_pad = deep_w.shape[1]
    plain = second_hbm.shape[1] - branch - deep_in
    margin = (row_hbm.shape[0] - 1) // 2

    def row_copy(h):
        return pltpu.make_async_copy(x_hbm.at[h], x_buf.at[h], x_sem.at[h])

    pairs = (
        (entry_hbm, entry_w),
        (row_hbm, row_w.at[:, 0:half]),
        (column_hbm, column_w.at[:, 0:half]),
        (wide_hbm, wide_w.at[:, 0:half]),
        (reduce_hbm, reduce_w.at[:, 0:half]),
        (second_hbm, second_w),
        (second_row_hbm, second_row_w),
        (second_column_hbm, second_column_w),
        (deep_hbm, deep_w.at[:, 0:deep_in]),
        (deep_row_hbm, deep_row_w),
        (deep_column_hbm, deep_column_w),
        (project_hbm, project_w),
    )
    copies = [
        pltpu.make_async_copy(source, target, w_sem.at[i])
        for i, (source, target) in enumerate(pairs)
    ]
    copies[0].start()
    for h in range(grid):
        row_copy(h).start()
    for ref in (wide_w, row_w, column_w, reduce_w):
        ref[:, half:] = jnp.zeros((ref.shape[0], half_pad - half, ref.shape[2]), ref.dtype)
    deep_w[:, deep_in:] = jnp.zeros(
        (deep_w.shape[0], deep_pad - deep_in, deep_w.shape[2]), deep_w.dtype
    )
    for copy in copies[1:]:
        copy.start()

    low = half // 128 * 128
    for ref in (short_buf, column_buf, tower_buf):
        ref[..., low:] = jnp.zeros(ref.shape[:3] + (ref.shape[3] - low,), ref.dtype)
    long_buf[..., low:] = jnp.zeros(long_buf.shape[:3] + (half_pad - low,), long_buf.dtype)
    for edge in (pl.ds(0, margin), pl.ds(grid + margin, margin)):
        long_buf[:, edge] = jnp.zeros((grid, margin, images, half_pad), long_buf.dtype)
        column_buf[edge] = jnp.zeros((margin, grid, images, half_pad), column_buf.dtype)
    deep_low = deep_in // 128 * 128
    deep_buf[..., deep_low:] = jnp.zeros(
        deep_buf.shape[:3] + (deep_pad - deep_low,), deep_buf.dtype
    )
    for ref in (mid_buf, branch_buf, deep_buf, deep_out_buf):
        line = jnp.zeros((small + 2, images, ref.shape[3]), ref.dtype)
        ref[0] = line
        ref[small + 1] = line
        ref[:, 0] = line
        ref[:, small + 1] = line

    copies[0].wait()

    tall = 4

    def by_rows(step_body):
        def looped(step, carry):
            step_body(step * tall, tall)
            return carry

        lax.fori_loop(0, grid // tall, looped, 0)
        if grid % tall:
            step_body(grid // tall * tall, grid % tall)

    def entry_step(h, n):
        for g in range(n):
            row_copy(h + g).wait()
        out = rectified(x_buf[pl.ds(h, n)].reshape(n * grid * images, in_ch), entry_w[...])
        short_buf[pl.ds(h, n), :, :, 0:half] = out[:, 0:half].reshape(n, grid, images, half)
        long_buf[pl.ds(h, n), pl.ds(margin, grid), :, 0:half] = out[:, half:].reshape(
            n, grid, images, half
        )

    by_rows(entry_step)

    copies[1].wait()

    def row_step(h, n):
        lhs = jnp.concatenate(
            [
                long_buf[pl.ds(h, n), pl.ds(j, grid)].reshape(n * grid * images, half_pad)
                for j in range(2 * margin + 1)
            ],
            axis=1,
        )
        out = rectified(lhs, row_w[...].reshape(-1, half))
        column_buf[pl.ds(h + margin, n), :, :, 0:half] = out.reshape(n, grid, images, half)

    by_rows(row_step)

    copies[2].wait()

    def column_step(h, n):
        lhs = jnp.concatenate(
            [
                column_buf[pl.ds(h + i, n)].reshape(n * grid * images, half_pad)
                for i in range(2 * margin + 1)
            ],
            axis=1,
        )
        out = rectified(lhs, column_w[...].reshape(-1, half))
        tower_buf[pl.ds(h, n), :, :, 0:half] = out.reshape(n, grid, images, half)

    by_rows(column_step)

    group = small
    n_groups = small // group

    def strided(ref, r, j):
        start, odd = j // 2, (j + 1) // 2
        width = ref.shape[3]
        return ref[r, pl.ds(start, 2 * small)].reshape(small, 2, images, width)[:, odd]

    def strided_taps(ref, h):
        return jnp.concatenate(
            [
                jnp.concatenate(
                    [strided(ref, 2 * (h + g) + i, j) for g in range(group)], axis=0
                ).reshape(group * small * images, half_pad)
                for i in range(3)
                for j in range(3)
            ],
            axis=1,
        )

    copies[3].wait()
    copies[4].wait()

    def middle_step(step, carry):
        h = step * group
        wide_out = rectified(strided_taps(short_buf, h), wide_w[...].reshape(-1, wide))
        tower_out = rectified(strided_taps(tower_buf, h), reduce_w[...].reshape(-1, half))
        both = jnp.concatenate([wide_out, tower_out], axis=1)
        mid_buf[pl.ds(h + 1, group), pl.ds(1, small), :, 0 : wide + half] = both.reshape(
            group, small, images, wide + half
        )
        for g in range(group):
            for lane in range(0, in_ch, 256):
                lanes = pl.ds(lane, 256)
                r = 2 * (h + g)
                lines = jnp.maximum(
                    jnp.maximum(x_buf[r, :, :, lanes], x_buf[r + 1, :, :, lanes]),
                    x_buf[r + 2, :, :, lanes],
                )
                even = lines[0 : 2 * small].reshape(small, 2, images, 256)
                late = lines[1 : 2 * small + 1].reshape(small, 2, images, 256)
                mid_buf[h + g + 1, pl.ds(1, small), :, pl.ds(wide + half + lane, 256)] = (
                    jnp.maximum(jnp.maximum(even[:, 0], even[:, 1]), late[:, 1])
                )
        return carry

    lax.fori_loop(0, n_groups, middle_step, 0)

    rows_m = group * small * images
    here = pl.ds(1, small)

    def total(out):
        width = out.shape[1]
        return jnp.sum(out.astype(jnp.float32).reshape(group * small, images, width), axis=0)

    copies[5].wait()

    def second_step(step, plain_sum):
        h = step * group
        lhs = mid_buf[pl.ds(h + 1, group), here].reshape(rows_m, mid_ch)
        out = rectified(lhs, second_w[...])
        branch_buf[pl.ds(h + 1, group), here] = out[:, plain : plain + branch].reshape(
            group, small, images, branch
        )
        deep_buf[pl.ds(h + 1, group), here, :, 0:deep_in] = out[:, plain + branch :].reshape(
            group, small, images, deep_in
        )
        return plain_sum + total(out[:, 0:plain])

    plain_sum = lax.fori_loop(
        0, n_groups, second_step, jnp.zeros((images, plain), jnp.float32)
    )

    def window(ref, h, rows, cols):
        return jnp.concatenate(
            [
                ref[pl.ds(h + i, group), pl.ds(j, small)].reshape(rows_m, ref.shape[3])
                for i in rows
                for j in cols
            ],
            axis=1,
        )

    def pair_step(source, row_weights, column_weights):
        out_ch = row_weights.shape[2]

        def step_body(step, sums):
            h = step * group
            row_out = rectified(
                window(source, h, (1,), (0, 1, 2)), row_weights[...].reshape(-1, out_ch)
            )
            column_out = rectified(
                window(source, h, (0, 1, 2), (1,)), column_weights[...].reshape(-1, out_ch)
            )
            return sums[0] + total(row_out), sums[1] + total(column_out)

        zero = jnp.zeros((images, out_ch), jnp.float32)
        return lax.fori_loop(0, n_groups, step_body, (zero, zero))

    copies[6].wait()
    copies[7].wait()
    row_a, column_a = pair_step(branch_buf, second_row_w, second_column_w)

    copies[8].wait()

    def deep_step(step, carry):
        h = step * group
        lhs = window(deep_buf, h, (0, 1, 2), (0, 1, 2))
        out = rectified(lhs, deep_w[...].reshape(9 * deep_pad, -1))
        deep_out_buf[pl.ds(h + 1, group), here] = out.reshape(
            group, small, images, out.shape[1]
        )
        return carry

    lax.fori_loop(0, n_groups, deep_step, 0)

    copies[9].wait()
    copies[10].wait()
    row_b, column_b = pair_step(deep_out_buf, deep_row_w, deep_column_w)

    def average_step(chunk, carry):
        lanes = pl.ds(pl.multiple_of(chunk * 128, 128), 128)
        across = []
        for r in range(small + 2):
            line = mid_buf[r, :, :, lanes].astype(jnp.float32)
            across.append(line[0:small] + line[1 : small + 1] + line[2 : small + 2])
        for h in range(small):
            high = 2 if h in (0, small - 1) else 3
            summed = across[h] + across[h + 1] + across[h + 2]
            average_buf[h, 0, :, lanes] = (summed[0] * (1.0 / (2 * high))).astype(jnp.bfloat16)
            average_buf[h, pl.ds(1, small - 2), :, lanes] = (
                summed[1 : small - 1] * (1.0 / (3 * high))
            ).astype(jnp.bfloat16)
            average_buf[h, small - 1, :, lanes] = (
                summed[small - 1] * (1.0 / (2 * high))
            ).astype(jnp.bfloat16)
        return carry

    lax.fori_loop(0, mid_ch // 128, average_step, 0)

    copies[11].wait()

    def project_step(step, pooled_sum):
        lhs = average_buf[pl.ds(step * group, group)].reshape(rows_m, mid_ch)
        out = lax.dot_general(
            lhs, project_w[...], (((1,), (1,)), ((), ())), preferred_element_type=jnp.float32
        )
        return pooled_sum + total(jnp.maximum(out, 0.0).astype(jnp.bfloat16))

    pooled = lax.fori_loop(
        0, n_groups, project_step, jnp.zeros((images, project_w.shape[0]), jnp.float32)
    )
    features = jnp.concatenate([plain_sum, row_a, column_a, row_b, column_b, pooled], axis=1)
    feats_ref[...] = features * (1.0 / (small * small))


def network(
    block_inputs,
    first_entry,
    first_wide,
    first_row,
    first_column,
    first_reduce,
    second_entry,
    second_row,
    second_column,
    second_deep,
    deep_row,
    deep_column,
    pool_project,
):
    def flat(kernel):
        return kernel.reshape((-1,) + kernel.shape[2:])

    x = jnp.transpose(block_inputs, (1, 2, 0, 3))
    grid, _, images, in_ch = x.shape
    small = (grid - 3) // 2 + 1
    half = first_row.shape[2]
    half_pad = -(-half // 256) * 256
    deep_in = second_deep.shape[2]
    deep_pad = -(-deep_in // 128) * 128
    margin = (first_row.shape[1] - 1) // 2
    mid_ch = second_entry.shape[2]
    branch = second_row.shape[2]
    deep_ch = second_deep.shape[3]
    operands = [
        x,
        first_entry[0, 0],
        flat(first_wide),
        flat(first_row),
        flat(first_column),
        flat(first_reduce),
        second_entry[0, 0],
        flat(second_row),
        flat(second_column),
        flat(second_deep),
        flat(deep_row),
        flat(deep_column),
        pool_project[0, 0].T,
    ]
    width = second_entry.shape[3] - branch - deep_in + 2 * branch + 2 * deep_ch
    width += pool_project.shape[3]

    def scratch(*shape):
        return pltpu.VMEM(shape, jnp.bfloat16)

    def weight_scratch(kernel, depth):
        return scratch(kernel.shape[0], depth, kernel.shape[2])

    edge = small + 2
    return pl.pallas_call(
        network_kernel,
        out_shape=jax.ShapeDtypeStruct((images, width), jnp.float32),
        in_specs=[pl.BlockSpec(memory_space=pl.ANY)] * len(operands),
        out_specs=pl.BlockSpec(memory_space=pltpu.VMEM),
        scratch_shapes=[
            scratch(*x.shape),
            scratch(*operands[1].shape),
            weight_scratch(operands[2], half_pad),
            weight_scratch(operands[3], half_pad),
            weight_scratch(operands[4], half_pad),
            weight_scratch(operands[5], half_pad),
            scratch(*operands[6].shape),
            scratch(*operands[7].shape),
            scratch(*operands[8].shape),
            weight_scratch(operands[9], deep_pad),
            scratch(*operands[10].shape),
            scratch(*operands[11].shape),
            scratch(*operands[12].shape),
            scratch(grid, grid, images, half_pad),
            scratch(grid, grid + 2 * margin, images, half_pad),
            scratch(grid + 2 * margin, grid, images, half_pad),
            scratch(grid, grid, images, half_pad),
            scratch(edge, edge, images, mid_ch),
            scratch(edge, edge, images, branch),
            scratch(edge, edge, images, deep_pad),
            scratch(edge, edge, images, deep_ch),
            scratch(small, small, images, mid_ch),
            pltpu.SemaphoreType.DMA((grid,)),
            pltpu.SemaphoreType.DMA((len(operands) - 1,)),
        ],
        compiler_params=pltpu.CompilerParams(vmem_limit_bytes=60 * 1024 * 1024),
        name="network",
    )(*operands)


def exchange_kernel(
    n_sample,
    n_col,
    feats_ref,
    mean_ref,
    cov_ref,
    cols,
    rows,
    sums_col,
    sums_sample,
    col_send,
    col_recv,
    row_send,
    row_recv,
    sum_send,
    sum_recv,
    cols_send,
    cols_recv,
    rows_send,
    rows_recv,
    total_send,
    total_recv,
):
    s = lax.axis_index("sample")
    c = lax.axis_index("col")
    images = feats_ref.shape[0]
    col_width = cols.shape[3]
    row_width = rows.shape[3]
    total_images = images * n_sample * n_col
    mesh_id = pl.DeviceIdType.MESH

    def col_at(index):
        return pl.ds(pl.multiple_of(index * col_width, 128), col_width)

    def row_at(index):
        return pl.ds(pl.multiple_of(index * row_width, 128), row_width)

    def send(source, target, send_sem, recv_sem, sample, col):
        copy = pltpu.make_async_remote_copy(
            src_ref=source,
            dst_ref=target,
            send_sem=send_sem,
            recv_sem=recv_sem,
            device_id=(sample, col),
            device_id_type=mesh_id,
        )
        copy.start()
        return copy

    barrier = pltpu.get_barrier_semaphore()
    for k in range(1, n_col):
        pl.semaphore_signal(
            barrier, inc=1, device_id=(s, lax.rem(c + k, n_col)), device_id_type=mesh_id
        )
    for k in range(1, n_sample):
        pl.semaphore_signal(
            barrier, inc=1, device_id=(lax.rem(s + k, n_sample), c), device_id_type=mesh_id
        )
    sums_col[c] = jnp.sum(feats_ref[...], axis=0, keepdims=True)
    cols[s, c] = feats_ref[:, col_at(c)]
    rows[s, c] = feats_ref[:, row_at(s)]
    pl.semaphore_wait(barrier, n_col - 1 + n_sample - 1)

    sends = []
    first_cols, first_sums, first_rows = [], [], []
    for k in range(1, n_col):
        to = lax.rem(c + k, n_col)
        first_cols.append(
            send(feats_ref.at[:, col_at(to)], cols.at[s, c], col_send.at[k], col_recv.at[k], s, to)
        )
        first_sums.append(
            send(sums_col.at[c], sums_col.at[c], sum_send.at[k], sum_recv.at[k], s, to)
        )
    for k in range(1, n_sample):
        to = lax.rem(s + k, n_sample)
        first_rows.append(
            send(feats_ref.at[:, row_at(to)], rows.at[s, c], row_send.at[k], row_recv.at[k], to, c)
        )
    for copy in first_rows:
        copy.wait_recv()
    second_rows = []
    for k in range(1, n_col):
        to = lax.rem(c + k, n_col)
        second_rows.append(
            send(rows.at[:, c], rows.at[:, c], rows_send.at[k], rows_recv.at[k], s, to)
        )
    for copy in first_cols:
        copy.wait_recv()
    second_cols = []
    for k in range(1, n_sample):
        to = lax.rem(s + k, n_sample)
        second_cols.append(
            send(cols.at[s], cols.at[s], cols_send.at[k], cols_recv.at[k], to, c)
        )
    for copy in first_sums:
        copy.wait_recv()
    sums_sample[s] = jnp.sum(sums_col[...], axis=0)
    second_sums = []
    for k in range(1, n_sample):
        to = lax.rem(s + k, n_sample)
        second_sums.append(
            send(sums_sample.at[s], sums_sample.at[s], total_send.at[k], total_recv.at[k], to, c)
        )
    for copy in second_sums:
        copy.wait_recv()
    mean_ref[...] = jnp.sum(sums_sample[...], axis=0) * (1.0 / total_images)
    for copy in second_rows:
        copy.wait_recv()
    row_values = rows[...].reshape(total_images, row_width) - mean_ref[:, row_at(s)]
    row_values = row_values.T
    row_high = row_values.astype(jnp.bfloat16)
    row_low = (row_values - row_high.astype(jnp.float32)).astype(jnp.bfloat16)
    for copy in second_cols:
        copy.wait_recv()
    col_values = cols[...].reshape(total_images, col_width) - mean_ref[:, col_at(c)]
    col_high = col_values.astype(jnp.bfloat16)
    col_low = (col_values - col_high.astype(jnp.float32)).astype(jnp.bfloat16)
    product = jnp.dot(row_high, col_low, preferred_element_type=jnp.float32)
    product += jnp.dot(row_low, col_high, preferred_element_type=jnp.float32)
    product += jnp.dot(row_high, col_high, preferred_element_type=jnp.float32)
    cov_ref[...] = product * (1.0 / (total_images - 1))
    for copy in first_cols + first_sums + first_rows + second_rows + second_cols + second_sums:
        copy.wait_send()


def exchange(features):
    n_sample = lax.axis_size("sample")
    n_col = lax.axis_size("col")
    images, width = features.shape
    row_width = width // n_sample
    col_width = width // n_col
    dma = pltpu.SemaphoreType.DMA
    vmem = pl.BlockSpec(memory_space=pltpu.VMEM)
    mean, covariance = pl.pallas_call(
        functools.partial(exchange_kernel, n_sample, n_col),
        out_shape=(
            jax.ShapeDtypeStruct((1, width), jnp.float32),
            jax.ShapeDtypeStruct((row_width, col_width), jnp.float32),
        ),
        in_specs=[vmem],
        out_specs=(vmem, vmem),
        scratch_shapes=[
            pltpu.VMEM((n_sample, n_col, images, col_width), jnp.float32),
            pltpu.VMEM((n_sample, n_col, images, row_width), jnp.float32),
            pltpu.VMEM((n_col, 1, width), jnp.float32),
            pltpu.VMEM((n_sample, 1, width), jnp.float32),
            dma((n_col,)),
            dma((n_col,)),
            dma((n_sample,)),
            dma((n_sample,)),
            dma((n_col,)),
            dma((n_col,)),
            dma((n_sample,)),
            dma((n_sample,)),
            dma((n_col,)),
            dma((n_col,)),
            dma((n_sample,)),
            dma((n_sample,)),
        ],
        compiler_params=pltpu.CompilerParams(
            collective_id=0, has_side_effects=True, vmem_limit_bytes=48 * 1024 * 1024
        ),
        name="exchange",
    )(features)
    return mean.reshape(width), covariance


def local(
    block_inputs,
    first_entry,
    first_wide,
    first_row,
    first_column,
    first_reduce,
    second_entry,
    second_row,
    second_column,
    second_deep,
    deep_row,
    deep_column,
    pool_project,
):
    features = network(
        block_inputs,
        first_entry,
        first_wide,
        first_row,
        first_column,
        first_reduce,
        second_entry,
        second_row,
        second_column,
        second_deep,
        deep_row,
        deep_column,
        pool_project,
    )
    return exchange(features)


def solution(mesh):
    placed = (
        P(("sample", "col"), None, None, None),
        P(),
        P(),
        P(),
        P(),
        P(),
        P(),
        P(),
        P(),
        P(),
        P(),
        P(),
        P(),
    )
    return jax.shard_map(
        local, mesh=mesh, in_specs=placed, out_specs=(P(), P("sample", "col")), check_vma=False
    )
```

```python
import functools

import jax
import jax.numpy as jnp
from jax import lax
from jax.experimental import pallas as pl
from jax.experimental.pallas import tpu as pltpu
from jax.sharding import PartitionSpec as P


def in_turn(steps, step_body, carry):
    for step in range(steps):
        carry = step_body(step, carry)
    return carry


def rectified(lhs, weights):
    out = jnp.dot(lhs, weights, preferred_element_type=jnp.float32)
    return jnp.maximum(out, 0.0).astype(jnp.bfloat16)


def network_kernel(
    x_hbm,
    entry_hbm,
    wide_hbm,
    row_hbm,
    column_hbm,
    reduce_hbm,
    second_hbm,
    second_row_hbm,
    second_column_hbm,
    deep_hbm,
    deep_row_hbm,
    deep_column_hbm,
    project_hbm,
    feats_ref,
    x_buf,
    entry_w,
    wide_w,
    row_w,
    column_w,
    reduce_w,
    second_w,
    second_row_w,
    second_column_w,
    deep_w,
    deep_row_w,
    deep_column_w,
    project_w,
    short_buf,
    long_buf,
    column_buf,
    tower_buf,
    mid_buf,
    branch_buf,
    deep_buf,
    deep_out_buf,
    average_buf,
    x_sem,
    w_sem,
):
    grid, _, images, in_ch = x_buf.shape
    half = row_hbm.shape[1]
    half_pad = row_w.shape[1]
    wide = wide_hbm.shape[2]
    small = mid_buf.shape[0] - 2
    mid_ch = mid_buf.shape[3]
    branch = second_row_hbm.shape[1]
    deep_in = deep_hbm.shape[1]
    deep_pad = deep_w.shape[1]
    plain = second_hbm.shape[1] - branch - deep_in
    margin = (row_hbm.shape[0] - 1) // 2

    def row_copy(h):
        return pltpu.make_async_copy(x_hbm.at[h], x_buf.at[h], x_sem.at[h])

    pairs = (
        (entry_hbm, entry_w),
        (row_hbm, row_w.at[:, 0:half]),
        (column_hbm, column_w.at[:, 0:half]),
        (wide_hbm, wide_w.at[:, 0:half]),
        (reduce_hbm, reduce_w.at[:, 0:half]),
        (second_hbm, second_w),
        (second_row_hbm, second_row_w),
        (second_column_hbm, second_column_w),
        (deep_hbm, deep_w.at[:, 0:deep_in]),
        (deep_row_hbm, deep_row_w),
        (deep_column_hbm, deep_column_w),
        (project_hbm, project_w),
    )
    copies = [
        pltpu.make_async_copy(source, target, w_sem.at[i])
        for i, (source, target) in enumerate(pairs)
    ]
    copies[0].start()
    for h in range(grid):
        row_copy(h).start()
    for ref in (wide_w, row_w, column_w, reduce_w):
        ref[:, half:] = jnp.zeros((ref.shape[0], half_pad - half, ref.shape[2]), ref.dtype)
    deep_w[:, deep_in:] = jnp.zeros(
        (deep_w.shape[0], deep_pad - deep_in, deep_w.shape[2]), deep_w.dtype
    )
    for copy in copies[1:]:
        copy.start()

    low = half // 128 * 128
    for ref in (short_buf, column_buf, tower_buf):
        ref[..., low:] = jnp.zeros(ref.shape[:3] + (ref.shape[3] - low,), ref.dtype)
    long_buf[..., low:] = jnp.zeros(long_buf.shape[:3] + (half_pad - low,), long_buf.dtype)
    for edge in (pl.ds(0, margin), pl.ds(grid + margin, margin)):
        long_buf[:, edge] = jnp.zeros((grid, margin, images, half_pad), long_buf.dtype)
        column_buf[edge] = jnp.zeros((margin, grid, images, half_pad), column_buf.dtype)
    deep_low = deep_in // 128 * 128
    deep_buf[..., deep_low:] = jnp.zeros(
        deep_buf.shape[:3] + (deep_pad - deep_low,), deep_buf.dtype
    )
    for ref in (mid_buf, branch_buf, deep_buf, deep_out_buf):
        line = jnp.zeros((small + 2, images, ref.shape[3]), ref.dtype)
        ref[0] = line
        ref[small + 1] = line
        ref[:, 0] = line
        ref[:, small + 1] = line

    copies[0].wait()

    tall = 4

    def by_rows(step_body):
        def looped(step, carry):
            step_body(step * tall, tall)
            return carry

        lax.fori_loop(0, grid // tall, looped, 0)
        if grid % tall:
            step_body(grid // tall * tall, grid % tall)

    def entry_step(h, n):
        for g in range(n):
            row_copy(h + g).wait()
        out = rectified(x_buf[pl.ds(h, n)].reshape(n * grid * images, in_ch), entry_w[...])
        short_buf[pl.ds(h, n), :, :, 0:half] = out[:, 0:half].reshape(n, grid, images, half)
        long_buf[pl.ds(h, n), pl.ds(margin, grid), :, 0:half] = out[:, half:].reshape(
            n, grid, images, half
        )

    by_rows(entry_step)

    copies[1].wait()

    def row_step(h, n):
        lhs = jnp.concatenate(
            [
                long_buf[pl.ds(h, n), pl.ds(j, grid)].reshape(n * grid * images, half_pad)
                for j in range(2 * margin + 1)
            ],
            axis=1,
        )
        out = rectified(lhs, row_w[...].reshape(-1, half))
        column_buf[pl.ds(h + margin, n), :, :, 0:half] = out.reshape(n, grid, images, half)

    by_rows(row_step)

    copies[2].wait()

    def column_step(h, n):
        lhs = jnp.concatenate(
            [
                column_buf[pl.ds(h + i, n)].reshape(n * grid * images, half_pad)
                for i in range(2 * margin + 1)
            ],
            axis=1,
        )
        out = rectified(lhs, column_w[...].reshape(-1, half))
        tower_buf[pl.ds(h, n), :, :, 0:half] = out.reshape(n, grid, images, half)

    by_rows(column_step)

    group = small
    n_groups = small // group

    def strided(ref, r, j):
        start, odd = j // 2, (j + 1) // 2
        width = ref.shape[3]
        return ref[r, pl.ds(start, 2 * small)].reshape(small, 2, images, width)[:, odd]

    def strided_taps(ref, h):
        return jnp.concatenate(
            [
                jnp.concatenate(
                    [strided(ref, 2 * (h + g) + i, j) for g in range(group)], axis=0
                ).reshape(group * small * images, half_pad)
                for i in range(3)
                for j in range(3)
            ],
            axis=1,
        )

    for copy in copies[3:]:
        copy.wait()

    def middle_step(step, carry):
        h = step * group
        wide_out = rectified(strided_taps(short_buf, h), wide_w[...].reshape(-1, wide))
        tower_out = rectified(strided_taps(tower_buf, h), reduce_w[...].reshape(-1, half))
        both = jnp.concatenate([wide_out, tower_out], axis=1)
        mid_buf[pl.ds(h + 1, group), pl.ds(1, small), :, 0 : wide + half] = both.reshape(
            group, small, images, wide + half
        )
        for g in range(group):
            for lane in range(0, in_ch, 256):
                lanes = pl.ds(lane, 256)
                r = 2 * (h + g)
                lines = jnp.maximum(
                    jnp.maximum(x_buf[r, :, :, lanes], x_buf[r + 1, :, :, lanes]),
                    x_buf[r + 2, :, :, lanes],
                )
                even = lines[0 : 2 * small].reshape(small, 2, images, 256)
                late = lines[1 : 2 * small + 1].reshape(small, 2, images, 256)
                mid_buf[h + g + 1, pl.ds(1, small), :, pl.ds(wide + half + lane, 256)] = (
                    jnp.maximum(jnp.maximum(even[:, 0], even[:, 1]), late[:, 1])
                )
        return carry

    in_turn(n_groups, middle_step, 0)

    rows_m = group * small * images
    here = pl.ds(1, small)

    def total(out):
        width = out.shape[1]
        return jnp.sum(out.astype(jnp.float32).reshape(group * small, images, width), axis=0)

    def second_step(step, plain_sum):
        h = step * group
        lhs = mid_buf[pl.ds(h + 1, group), here].reshape(rows_m, mid_ch)
        out = rectified(lhs, second_w[...])
        branch_buf[pl.ds(h + 1, group), here] = out[:, plain : plain + branch].reshape(
            group, small, images, branch
        )
        deep_buf[pl.ds(h + 1, group), here, :, 0:deep_in] = out[:, plain + branch :].reshape(
            group, small, images, deep_in
        )
        return plain_sum + total(out[:, 0:plain])

    plain_sum = in_turn(
        n_groups, second_step, jnp.zeros((images, plain), jnp.float32)
    )

    def window(ref, h, rows, cols):
        return jnp.concatenate(
            [
                ref[pl.ds(h + i, group), pl.ds(j, small)].reshape(rows_m, ref.shape[3])
                for i in rows
                for j in cols
            ],
            axis=1,
        )

    def pair_step(source, row_weights, column_weights):
        out_ch = row_weights.shape[2]

        def step_body(step, sums):
            h = step * group
            row_out = rectified(
                window(source, h, (1,), (0, 1, 2)), row_weights[...].reshape(-1, out_ch)
            )
            column_out = rectified(
                window(source, h, (0, 1, 2), (1,)), column_weights[...].reshape(-1, out_ch)
            )
            return sums[0] + total(row_out), sums[1] + total(column_out)

        zero = jnp.zeros((images, out_ch), jnp.float32)
        return in_turn(n_groups, step_body, (zero, zero))

    row_a, column_a = pair_step(branch_buf, second_row_w, second_column_w)

    def deep_step(step, carry):
        h = step * group
        lhs = window(deep_buf, h, (0, 1, 2), (0, 1, 2))
        out = rectified(lhs, deep_w[...].reshape(9 * deep_pad, -1))
        deep_out_buf[pl.ds(h + 1, group), here] = out.reshape(
            group, small, images, out.shape[1]
        )
        return carry

    in_turn(n_groups, deep_step, 0)

    row_b, column_b = pair_step(deep_out_buf, deep_row_w, deep_column_w)

    def average_step(chunk, carry):
        lanes = pl.ds(chunk * 128, 128)
        across = []
        for r in range(small + 2):
            line = mid_buf[r, :, :, lanes].astype(jnp.float32)
            across.append(line[0:small] + line[1 : small + 1] + line[2 : small + 2])
        for h in range(small):
            high = 2 if h in (0, small - 1) else 3
            summed = across[h] + across[h + 1] + across[h + 2]
            average_buf[h, 0, :, lanes] = (summed[0] * (1.0 / (2 * high))).astype(jnp.bfloat16)
            average_buf[h, pl.ds(1, small - 2), :, lanes] = (
                summed[1 : small - 1] * (1.0 / (3 * high))
            ).astype(jnp.bfloat16)
            average_buf[h, small - 1, :, lanes] = (
                summed[small - 1] * (1.0 / (2 * high))
            ).astype(jnp.bfloat16)
        return carry

    in_turn(mid_ch // 128, average_step, 0)

    def project_step(step, pooled_sum):
        lhs = average_buf[pl.ds(step * group, group)].reshape(rows_m, mid_ch)
        out = lax.dot_general(
            lhs, project_w[...], (((1,), (1,)), ((), ())), preferred_element_type=jnp.float32
        )
        return pooled_sum + total(jnp.maximum(out, 0.0).astype(jnp.bfloat16))

    pooled = in_turn(
        n_groups, project_step, jnp.zeros((images, project_w.shape[0]), jnp.float32)
    )
    features = jnp.concatenate([plain_sum, row_a, column_a, row_b, column_b, pooled], axis=1)
    feats_ref[...] = features * (1.0 / (small * small))


def network(
    block_inputs,
    first_entry,
    first_wide,
    first_row,
    first_column,
    first_reduce,
    second_entry,
    second_row,
    second_column,
    second_deep,
    deep_row,
    deep_column,
    pool_project,
):
    def flat(kernel):
        return kernel.reshape((-1,) + kernel.shape[2:])

    x = jnp.transpose(block_inputs, (1, 2, 0, 3))
    grid, _, images, in_ch = x.shape
    small = (grid - 3) // 2 + 1
    half = first_row.shape[2]
    half_pad = -(-half // 256) * 256
    deep_in = second_deep.shape[2]
    deep_pad = -(-deep_in // 128) * 128
    margin = (first_row.shape[1] - 1) // 2
    mid_ch = second_entry.shape[2]
    branch = second_row.shape[2]
    deep_ch = second_deep.shape[3]
    operands = [
        x,
        first_entry[0, 0],
        flat(first_wide),
        flat(first_row),
        flat(first_column),
        flat(first_reduce),
        second_entry[0, 0],
        flat(second_row),
        flat(second_column),
        flat(second_deep),
        flat(deep_row),
        flat(deep_column),
        pool_project[0, 0].T,
    ]
    width = second_entry.shape[3] - branch - deep_in + 2 * branch + 2 * deep_ch
    width += pool_project.shape[3]

    def scratch(*shape):
        return pltpu.VMEM(shape, jnp.bfloat16)

    def weight_scratch(kernel, depth):
        return scratch(kernel.shape[0], depth, kernel.shape[2])

    edge = small + 2
    return pl.pallas_call(
        network_kernel,
        out_shape=jax.ShapeDtypeStruct((images, width), jnp.float32),
        in_specs=[pl.BlockSpec(memory_space=pl.ANY)] * len(operands),
        out_specs=pl.BlockSpec(memory_space=pltpu.VMEM),
        scratch_shapes=[
            scratch(*x.shape),
            scratch(*operands[1].shape),
            weight_scratch(operands[2], half_pad),
            weight_scratch(operands[3], half_pad),
            weight_scratch(operands[4], half_pad),
            weight_scratch(operands[5], half_pad),
            scratch(*operands[6].shape),
            scratch(*operands[7].shape),
            scratch(*operands[8].shape),
            weight_scratch(operands[9], deep_pad),
            scratch(*operands[10].shape),
            scratch(*operands[11].shape),
            scratch(*operands[12].shape),
            scratch(grid, grid, images, half_pad),
            scratch(grid, grid + 2 * margin, images, half_pad),
            scratch(grid + 2 * margin, grid, images, half_pad),
            scratch(grid, grid, images, half_pad),
            scratch(edge, edge, images, mid_ch),
            scratch(edge, edge, images, branch),
            scratch(edge, edge, images, deep_pad),
            scratch(edge, edge, images, deep_ch),
            scratch(small, small, images, mid_ch),
            pltpu.SemaphoreType.DMA((grid,)),
            pltpu.SemaphoreType.DMA((len(operands) - 1,)),
        ],
        compiler_params=pltpu.CompilerParams(vmem_limit_bytes=60 * 1024 * 1024),
        name="network",
    )(*operands)


def exchange_kernel(
    n_sample,
    n_col,
    feats_hbm,
    mean_ref,
    cov_ref,
    feats_ref,
    cols_high,
    cols_low,
    cols,
    rows,
    sums_col,
    sums_sample,
    col_send,
    col_recv,
    row_send,
    row_recv,
    sum_send,
    sum_recv,
    cols_send,
    cols_recv,
    rows_send,
    rows_recv,
    total_send,
    total_recv,
    pair_send,
    pair_recv,
    fetch_sem,
):
    s = lax.axis_index("sample")
    c = lax.axis_index("col")
    images = feats_ref.shape[0]
    col_width = cols.shape[3]
    row_width = rows.shape[3]
    total_images = images * n_sample * n_col
    mesh_id = pl.DeviceIdType.MESH

    def col_at(index):
        return pl.ds(pl.multiple_of(index * col_width, 128), col_width)

    def row_at(index):
        return pl.ds(pl.multiple_of(index * row_width, 128), row_width)

    def send(source, target, send_sem, recv_sem, sample, col):
        copy = pltpu.make_async_remote_copy(
            src_ref=source,
            dst_ref=target,
            send_sem=send_sem,
            recv_sem=recv_sem,
            device_id=(sample, col),
            device_id_type=mesh_id,
        )
        copy.start()
        return copy

    fetch = pltpu.make_async_copy(feats_hbm, feats_ref, fetch_sem)
    fetch.start()
    barrier = pltpu.get_barrier_semaphore()
    for k in range(1, n_col):
        pl.semaphore_signal(
            barrier, inc=1, device_id=(s, lax.rem(c + k, n_col)), device_id_type=mesh_id
        )
    for k in range(1, n_sample):
        pl.semaphore_signal(
            barrier, inc=1, device_id=(lax.rem(s + k, n_sample), c), device_id_type=mesh_id
        )
    fetch.wait()
    sums_col[c] = jnp.sum(feats_ref[...], axis=0, keepdims=True)
    cols[s, c] = feats_ref[:, col_at(c)]
    rows[s, c] = feats_ref[:, row_at(s)]
    pl.semaphore_wait(barrier, n_col - 1 + n_sample - 1)

    first_cols, first_sums, first_rows = [], [], []
    for k in range(1, n_col):
        to = lax.rem(c + k, n_col)
        first_sums.append(
            send(sums_col.at[c], sums_col.at[c], sum_send.at[k], sum_recv.at[k], s, to)
        )
        first_cols.append(
            send(feats_ref.at[:, col_at(to)], cols.at[s, c], col_send.at[k], col_recv.at[k], s, to)
        )
    for k in range(1, n_sample):
        to = lax.rem(s + k, n_sample)
        first_rows.append(
            send(feats_ref.at[:, row_at(to)], rows.at[s, c], row_send.at[k], row_recv.at[k], to, c)
        )

    pair = 2 if n_sample % 2 == 0 else 1
    n_pairs = n_sample // pair
    mine = lax.rem(s, pair)
    sibling = s + 1 - 2 * mine

    def same_side(k):
        return lax.rem(s // pair + k + n_pairs, n_pairs) * pair + mine

    def hand_on(slot, k):
        return send(cols.at[slot], cols.at[slot], pair_send.at[k], pair_recv.at[k], sibling, c)

    def hop(plane, to, index):
        return pltpu.make_async_remote_copy(
            src_ref=rows.at[:, plane],
            dst_ref=rows.at[:, plane],
            send_sem=rows_send.at[index],
            recv_sem=rows_recv.at[index],
            device_id=(s, to),
            device_id_type=mesh_id,
        )

    def send_right(k):
        return (c + 1 < n_col) & (c >= k - 1)

    def send_left(k):
        return (c >= 1) & (c + k - 1 < n_col)

    def right(k):
        return hop(lax.rem(c - k + 1 + n_col, n_col), lax.rem(c + 1, n_col), k)

    def left(k):
        return hop(lax.rem(c + k - 1, n_col), lax.rem(c - 1 + n_col, n_col), n_col + k)

    def start_hops(k):
        @pl.when(send_right(k))
        def _():
            right(k).start()

        @pl.when(send_left(k))
        def _():
            left(k).start()

    def finish_hops(k):
        @pl.when(c >= k)
        def _():
            right(k).wait_recv()

        @pl.when(c + k < n_col)
        def _():
            left(k).wait_recv()

    for copy in first_sums:
        copy.wait_recv()
    sums_sample[s] = jnp.sum(sums_col[...], axis=0)
    second_sums = []
    for k in range(1, n_sample):
        to = lax.rem(s + k, n_sample)
        second_sums.append(
            send(sums_sample.at[s], sums_sample.at[s], total_send.at[k], total_recv.at[k], to, c)
        )
    for copy in first_rows:
        copy.wait_recv()
    start_hops(1)
    for copy in first_cols:
        copy.wait_recv()
    second_cols = []
    for k in range(1, n_pairs):
        second_cols.append(
            send(cols.at[s], cols.at[s], cols_send.at[k], cols_recv.at[k], same_side(k), c)
        )
    handed = [hand_on(s, 0)] if pair == 2 else []
    for copy in second_sums:
        copy.wait_recv()
    mean_ref[...] = jnp.sum(sums_sample[...], axis=0) * (1.0 / total_images)

    def prepare(slot):
        values = cols[slot].reshape(n_col * images, col_width) - mean_ref[:, col_at(c)]
        high = values.astype(jnp.bfloat16)
        cols_high[slot] = high
        cols_low[slot] = (values - high.astype(jnp.float32)).astype(jnp.bfloat16)

    prepare(s)
    for k in range(1, max(n_col, n_pairs)):
        if k < n_pairs:
            second_cols[k - 1].wait_recv()
            if pair == 2:
                handed.append(hand_on(same_side(-k), k))
        if k < n_col:
            finish_hops(k)
            if k + 1 < n_col:
                start_hops(k + 1)
        if k < n_pairs:
            prepare(same_side(-k))
    for k, copy in enumerate(handed):
        copy.wait_recv()
        prepare(same_side(-k) + 1 - 2 * mine)
    row_values = rows[...].reshape(total_images, row_width) - mean_ref[:, row_at(s)]
    row_values = row_values.T
    row_high = row_values.astype(jnp.bfloat16)
    row_low = (row_values - row_high.astype(jnp.float32)).astype(jnp.bfloat16)
    col_high = cols_high[...].reshape(total_images, col_width)
    col_low = cols_low[...].reshape(total_images, col_width)
    product = jnp.dot(row_high, col_low, preferred_element_type=jnp.float32)
    product += jnp.dot(row_low, col_high, preferred_element_type=jnp.float32)
    product += jnp.dot(row_high, col_high, preferred_element_type=jnp.float32)
    cov_ref[...] = product * (1.0 / (total_images - 1))
    for copy in first_cols + first_sums + first_rows + second_cols + second_sums + handed:
        copy.wait_send()
    for k in range(1, n_col):

        @pl.when(send_right(k))
        def _():
            right(k).wait_send()

        @pl.when(send_left(k))
        def _():
            left(k).wait_send()


def exchange(features):
    n_sample = lax.axis_size("sample")
    n_col = lax.axis_size("col")
    images, width = features.shape
    row_width = width // n_sample
    col_width = width // n_col
    dma = pltpu.SemaphoreType.DMA
    vmem = pl.BlockSpec(memory_space=pltpu.VMEM)
    mean, covariance = pl.pallas_call(
        functools.partial(exchange_kernel, n_sample, n_col),
        out_shape=(
            jax.ShapeDtypeStruct((1, width), jnp.float32),
            jax.ShapeDtypeStruct((row_width, col_width), jnp.float32),
        ),
        in_specs=[pl.BlockSpec(memory_space=pl.ANY)],
        out_specs=(vmem, vmem),
        scratch_shapes=[
            pltpu.VMEM((images, width), jnp.float32),
            pltpu.VMEM((n_sample, n_col * images, col_width), jnp.bfloat16),
            pltpu.VMEM((n_sample, n_col * images, col_width), jnp.bfloat16),
            pltpu.VMEM((n_sample, n_col, images, col_width), jnp.float32),
            pltpu.VMEM((n_sample, n_col, images, row_width), jnp.float32),
            pltpu.VMEM((n_col, 1, width), jnp.float32),
            pltpu.VMEM((n_sample, 1, width), jnp.float32),
            dma((n_col,)),
            dma((n_col,)),
            dma((n_sample,)),
            dma((n_sample,)),
            dma((n_col,)),
            dma((n_col,)),
            dma((n_sample,)),
            dma((n_sample,)),
            dma((2 * n_col,)),
            dma((2 * n_col,)),
            dma((n_sample,)),
            dma((n_sample,)),
            dma((n_sample,)),
            dma((n_sample,)),
            dma,
        ],
        compiler_params=pltpu.CompilerParams(
            collective_id=0, has_side_effects=True, vmem_limit_bytes=48 * 1024 * 1024
        ),
        name="exchange",
    )(features)
    return mean.reshape(width), covariance


def local(
    block_inputs,
    first_entry,
    first_wide,
    first_row,
    first_column,
    first_reduce,
    second_entry,
    second_row,
    second_column,
    second_deep,
    deep_row,
    deep_column,
    pool_project,
):
    features = network(
        block_inputs,
        first_entry,
        first_wide,
        first_row,
        first_column,
        first_reduce,
        second_entry,
        second_row,
        second_column,
        second_deep,
        deep_row,
        deep_column,
        pool_project,
    )
    return exchange(features)


def solution(mesh):
    placed = (
        P(("sample", "col"), None, None, None),
        P(),
        P(),
        P(),
        P(),
        P(),
        P(),
        P(),
        P(),
        P(),
        P(),
        P(),
        P(),
    )
    return jax.shard_map(
        local, mesh=mesh, in_specs=placed, out_specs=(P(), P("sample", "col")), check_vma=False
    )
```

```python
import functools

import jax
import jax.numpy as jnp
from jax import lax
from jax.experimental import pallas as pl
from jax.experimental.pallas import tpu as pltpu
from jax.sharding import PartitionSpec as P


def in_turn(steps, step_body, carry):
    for step in range(steps):
        carry = step_body(step, carry)
    return carry


def rectified(lhs, weights):
    out = jnp.dot(lhs, weights, preferred_element_type=jnp.float32)
    return jnp.maximum(out, 0.0).astype(jnp.bfloat16)


def network_kernel(
    x_hbm,
    entry_hbm,
    wide_hbm,
    row_hbm,
    column_hbm,
    reduce_hbm,
    second_hbm,
    second_row_hbm,
    second_column_hbm,
    deep_hbm,
    deep_row_hbm,
    deep_column_hbm,
    project_hbm,
    feats_ref,
    x_buf,
    entry_w,
    wide_w,
    row_w,
    column_w,
    reduce_w,
    second_w,
    second_row_w,
    second_column_w,
    deep_w,
    deep_row_w,
    deep_column_w,
    project_w,
    short_buf,
    long_buf,
    column_buf,
    tower_buf,
    mid_buf,
    branch_buf,
    deep_buf,
    deep_out_buf,
    average_buf,
    x_sem,
    w_sem,
):
    grid, _, images, in_ch = x_buf.shape
    half = row_hbm.shape[1]
    half_pad = row_w.shape[1]
    wide = wide_hbm.shape[2]
    small = mid_buf.shape[0] - 2
    mid_ch = mid_buf.shape[3]
    branch = second_row_hbm.shape[1]
    deep_in = deep_hbm.shape[1]
    deep_pad = deep_w.shape[1]
    plain = second_hbm.shape[1] - branch - deep_in
    margin = (row_hbm.shape[0] - 1) // 2

    def row_copy(h):
        return pltpu.make_async_copy(x_hbm.at[h], x_buf.at[h], x_sem.at[h])

    pairs = (
        (entry_hbm, entry_w),
        (row_hbm, row_w.at[:, 0:half]),
        (column_hbm, column_w.at[:, 0:half]),
        (wide_hbm, wide_w.at[:, 0:half]),
        (reduce_hbm, reduce_w.at[:, 0:half]),
        (second_hbm, second_w),
        (second_row_hbm, second_row_w),
        (second_column_hbm, second_column_w),
        (deep_hbm, deep_w.at[:, 0:deep_in]),
        (deep_row_hbm, deep_row_w),
        (deep_column_hbm, deep_column_w),
        (project_hbm, project_w),
    )
    copies = [
        pltpu.make_async_copy(source, target, w_sem.at[i])
        for i, (source, target) in enumerate(pairs)
    ]
    copies[0].start()
    for h in range(grid):
        row_copy(h).start()
    for ref in (wide_w, row_w, column_w, reduce_w):
        ref[:, half:] = jnp.zeros((ref.shape[0], half_pad - half, ref.shape[2]), ref.dtype)
    deep_w[:, deep_in:] = jnp.zeros(
        (deep_w.shape[0], deep_pad - deep_in, deep_w.shape[2]), deep_w.dtype
    )
    for copy in copies[1:]:
        copy.start()

    low = half // 128 * 128
    for ref in (short_buf, column_buf, tower_buf):
        ref[..., low:] = jnp.zeros(ref.shape[:3] + (ref.shape[3] - low,), ref.dtype)
    long_buf[..., low:] = jnp.zeros(long_buf.shape[:3] + (half_pad - low,), long_buf.dtype)
    for edge in (pl.ds(0, margin), pl.ds(grid + margin, margin)):
        long_buf[:, edge] = jnp.zeros((grid, margin, images, half_pad), long_buf.dtype)
        column_buf[edge] = jnp.zeros((margin, grid, images, half_pad), column_buf.dtype)
    deep_low = deep_in // 128 * 128
    deep_buf[..., deep_low:] = jnp.zeros(
        deep_buf.shape[:3] + (deep_pad - deep_low,), deep_buf.dtype
    )
    for ref in (mid_buf, branch_buf, deep_buf, deep_out_buf):
        line = jnp.zeros((small + 2, images, ref.shape[3]), ref.dtype)
        ref[0] = line
        ref[small + 1] = line
        ref[:, 0] = line
        ref[:, small + 1] = line

    copies[0].wait()

    def by_rows(step_body, tall):
        def looped(step, carry):
            step_body(step * tall, tall)
            return carry

        lax.fori_loop(0, grid // tall, looped, 0)
        if grid % tall:
            step_body(grid // tall * tall, grid % tall)

    def entry_step(h, n):
        for g in range(n):
            row_copy(h + g).wait()
        out = rectified(x_buf[pl.ds(h, n)].reshape(n * grid * images, in_ch), entry_w[...])
        short_buf[pl.ds(h, n), :, :, 0:half] = out[:, 0:half].reshape(n, grid, images, half)
        long_buf[pl.ds(h, n), pl.ds(margin, grid), :, 0:half] = out[:, half:].reshape(
            n, grid, images, half
        )

    by_rows(entry_step, 4)

    copies[1].wait()

    def row_step(h, n):
        lhs = jnp.concatenate(
            [
                long_buf[pl.ds(h, n), pl.ds(j, grid)].reshape(n * grid * images, half_pad)
                for j in range(2 * margin + 1)
            ],
            axis=1,
        )
        out = rectified(lhs, row_w[...].reshape(-1, half))
        column_buf[pl.ds(h + margin, n), :, :, 0:half] = out.reshape(n, grid, images, half)

    by_rows(row_step, 8)

    copies[2].wait()

    def column_step(h, n):
        lhs = jnp.concatenate(
            [
                column_buf[pl.ds(h + i, n)].reshape(n * grid * images, half_pad)
                for i in range(2 * margin + 1)
            ],
            axis=1,
        )
        out = rectified(lhs, column_w[...].reshape(-1, half))
        tower_buf[pl.ds(h, n), :, :, 0:half] = out.reshape(n, grid, images, half)

    by_rows(column_step, 8)

    group = small
    n_groups = small // group

    def strided(ref, r, j):
        start, odd = j // 2, (j + 1) // 2
        width = ref.shape[3]
        return ref[r, pl.ds(start, 2 * small)].reshape(small, 2, images, width)[:, odd]

    def strided_taps(ref, h):
        return jnp.concatenate(
            [
                jnp.concatenate(
                    [strided(ref, 2 * (h + g) + i, j) for g in range(group)], axis=0
                ).reshape(group * small * images, half_pad)
                for i in range(3)
                for j in range(3)
            ],
            axis=1,
        )

    for copy in copies[3:]:
        copy.wait()

    def middle_step(step, carry):
        h = step * group
        wide_out = rectified(strided_taps(short_buf, h), wide_w[...].reshape(-1, wide))
        tower_out = rectified(strided_taps(tower_buf, h), reduce_w[...].reshape(-1, half))
        both = jnp.concatenate([wide_out, tower_out], axis=1)
        mid_buf[pl.ds(h + 1, group), pl.ds(1, small), :, 0 : wide + half] = both.reshape(
            group, small, images, wide + half
        )
        for g in range(group):
            for lane in range(0, in_ch, 256):
                lanes = pl.ds(lane, 256)
                r = 2 * (h + g)
                lines = jnp.maximum(
                    jnp.maximum(x_buf[r, :, :, lanes], x_buf[r + 1, :, :, lanes]),
                    x_buf[r + 2, :, :, lanes],
                )
                even = lines[0 : 2 * small].reshape(small, 2, images, 256)
                late = lines[1 : 2 * small + 1].reshape(small, 2, images, 256)
                mid_buf[h + g + 1, pl.ds(1, small), :, pl.ds(wide + half + lane, 256)] = (
                    jnp.maximum(jnp.maximum(even[:, 0], even[:, 1]), late[:, 1])
                )
        return carry

    in_turn(n_groups, middle_step, 0)

    rows_m = group * small * images
    here = pl.ds(1, small)

    def total(out):
        width = out.shape[1]
        return jnp.sum(out.astype(jnp.float32).reshape(group * small, images, width), axis=0)

    def second_step(step, plain_sum):
        h = step * group
        lhs = mid_buf[pl.ds(h + 1, group), here].reshape(rows_m, mid_ch)
        out = rectified(lhs, second_w[...])
        branch_buf[pl.ds(h + 1, group), here] = out[:, plain : plain + branch].reshape(
            group, small, images, branch
        )
        deep_buf[pl.ds(h + 1, group), here, :, 0:deep_in] = out[:, plain + branch :].reshape(
            group, small, images, deep_in
        )
        return plain_sum + total(out[:, 0:plain])

    plain_sum = in_turn(
        n_groups, second_step, jnp.zeros((images, plain), jnp.float32)
    )

    def window(ref, h, rows, cols):
        return jnp.concatenate(
            [
                ref[pl.ds(h + i, group), pl.ds(j, small)].reshape(rows_m, ref.shape[3])
                for i in rows
                for j in cols
            ],
            axis=1,
        )

    def pair_step(source, row_weights, column_weights):
        out_ch = row_weights.shape[2]

        def step_body(step, sums):
            h = step * group
            row_out = rectified(
                window(source, h, (1,), (0, 1, 2)), row_weights[...].reshape(-1, out_ch)
            )
            column_out = rectified(
                window(source, h, (0, 1, 2), (1,)), column_weights[...].reshape(-1, out_ch)
            )
            return sums[0] + total(row_out), sums[1] + total(column_out)

        zero = jnp.zeros((images, out_ch), jnp.float32)
        return in_turn(n_groups, step_body, (zero, zero))

    row_a, column_a = pair_step(branch_buf, second_row_w, second_column_w)

    def deep_step(step, carry):
        h = step * group
        lhs = window(deep_buf, h, (0, 1, 2), (0, 1, 2))
        out = rectified(lhs, deep_w[...].reshape(9 * deep_pad, -1))
        deep_out_buf[pl.ds(h + 1, group), here] = out.reshape(
            group, small, images, out.shape[1]
        )
        return carry

    in_turn(n_groups, deep_step, 0)

    row_b, column_b = pair_step(deep_out_buf, deep_row_w, deep_column_w)

    def average_step(chunk, carry):
        lanes = pl.ds(chunk * 128, 128)
        across = []
        for r in range(small + 2):
            line = mid_buf[r, :, :, lanes].astype(jnp.float32)
            across.append(line[0:small] + line[1 : small + 1] + line[2 : small + 2])
        for h in range(small):
            high = 2 if h in (0, small - 1) else 3
            summed = across[h] + across[h + 1] + across[h + 2]
            average_buf[h, 0, :, lanes] = (summed[0] * (1.0 / (2 * high))).astype(jnp.bfloat16)
            average_buf[h, pl.ds(1, small - 2), :, lanes] = (
                summed[1 : small - 1] * (1.0 / (3 * high))
            ).astype(jnp.bfloat16)
            average_buf[h, small - 1, :, lanes] = (
                summed[small - 1] * (1.0 / (2 * high))
            ).astype(jnp.bfloat16)
        return carry

    in_turn(mid_ch // 128, average_step, 0)

    def project_step(step, pooled_sum):
        lhs = average_buf[pl.ds(step * group, group)].reshape(rows_m, mid_ch)
        out = lax.dot_general(
            lhs, project_w[...], (((1,), (1,)), ((), ())), preferred_element_type=jnp.float32
        )
        return pooled_sum + total(jnp.maximum(out, 0.0).astype(jnp.bfloat16))

    pooled = in_turn(
        n_groups, project_step, jnp.zeros((images, project_w.shape[0]), jnp.float32)
    )
    features = jnp.concatenate([plain_sum, row_a, column_a, row_b, column_b, pooled], axis=1)
    feats_ref[...] = features * (1.0 / (small * small))


def network(
    block_inputs,
    first_entry,
    first_wide,
    first_row,
    first_column,
    first_reduce,
    second_entry,
    second_row,
    second_column,
    second_deep,
    deep_row,
    deep_column,
    pool_project,
):
    def flat(kernel):
        return kernel.reshape((-1,) + kernel.shape[2:])

    x = jnp.transpose(block_inputs, (1, 2, 0, 3))
    grid, _, images, in_ch = x.shape
    small = (grid - 3) // 2 + 1
    half = first_row.shape[2]
    half_pad = -(-half // 256) * 256
    deep_in = second_deep.shape[2]
    deep_pad = -(-deep_in // 128) * 128
    margin = (first_row.shape[1] - 1) // 2
    mid_ch = second_entry.shape[2]
    branch = second_row.shape[2]
    deep_ch = second_deep.shape[3]
    operands = [
        x,
        first_entry[0, 0],
        flat(first_wide),
        flat(first_row),
        flat(first_column),
        flat(first_reduce),
        second_entry[0, 0],
        flat(second_row),
        flat(second_column),
        flat(second_deep),
        flat(deep_row),
        flat(deep_column),
        pool_project[0, 0].T,
    ]
    width = second_entry.shape[3] - branch - deep_in + 2 * branch + 2 * deep_ch
    width += pool_project.shape[3]

    def scratch(*shape):
        return pltpu.VMEM(shape, jnp.bfloat16)

    def weight_scratch(kernel, depth):
        return scratch(kernel.shape[0], depth, kernel.shape[2])

    edge = small + 2
    return pl.pallas_call(
        network_kernel,
        out_shape=jax.ShapeDtypeStruct((images, width), jnp.float32),
        in_specs=[pl.BlockSpec(memory_space=pl.ANY)] * len(operands),
        out_specs=pl.BlockSpec(memory_space=pltpu.VMEM),
        scratch_shapes=[
            scratch(*x.shape),
            scratch(*operands[1].shape),
            weight_scratch(operands[2], half_pad),
            weight_scratch(operands[3], half_pad),
            weight_scratch(operands[4], half_pad),
            weight_scratch(operands[5], half_pad),
            scratch(*operands[6].shape),
            scratch(*operands[7].shape),
            scratch(*operands[8].shape),
            weight_scratch(operands[9], deep_pad),
            scratch(*operands[10].shape),
            scratch(*operands[11].shape),
            scratch(*operands[12].shape),
            scratch(grid, grid, images, half_pad),
            scratch(grid, grid + 2 * margin, images, half_pad),
            scratch(grid + 2 * margin, grid, images, half_pad),
            scratch(grid, grid, images, half_pad),
            scratch(edge, edge, images, mid_ch),
            scratch(edge, edge, images, branch),
            scratch(edge, edge, images, deep_pad),
            scratch(edge, edge, images, deep_ch),
            scratch(small, small, images, mid_ch),
            pltpu.SemaphoreType.DMA((grid,)),
            pltpu.SemaphoreType.DMA((len(operands) - 1,)),
        ],
        compiler_params=pltpu.CompilerParams(vmem_limit_bytes=60 * 1024 * 1024),
        name="network",
    )(*operands)


def exchange_kernel(
    n_sample,
    n_col,
    feats_hbm,
    mean_ref,
    cov_ref,
    feats_ref,
    cols_high,
    cols_low,
    cols,
    rows,
    sums_col,
    sums_sample,
    col_send,
    col_recv,
    row_send,
    row_recv,
    sum_send,
    sum_recv,
    cols_send,
    cols_recv,
    rows_send,
    rows_recv,
    total_send,
    total_recv,
    pair_send,
    pair_recv,
    fetch_sem,
):
    s = lax.axis_index("sample")
    c = lax.axis_index("col")
    images = feats_ref.shape[0]
    col_width = cols.shape[3]
    row_width = rows.shape[3]
    total_images = images * n_sample * n_col
    mesh_id = pl.DeviceIdType.MESH

    def col_at(index):
        return pl.ds(pl.multiple_of(index * col_width, 128), col_width)

    def row_at(index):
        return pl.ds(pl.multiple_of(index * row_width, 128), row_width)

    def send(source, target, send_sem, recv_sem, sample, col):
        copy = pltpu.make_async_remote_copy(
            src_ref=source,
            dst_ref=target,
            send_sem=send_sem,
            recv_sem=recv_sem,
            device_id=(sample, col),
            device_id_type=mesh_id,
        )
        copy.start()
        return copy

    fetch = pltpu.make_async_copy(feats_hbm, feats_ref, fetch_sem)
    fetch.start()
    barrier = pltpu.get_barrier_semaphore()
    for k in range(1, n_col):
        pl.semaphore_signal(
            barrier, inc=1, device_id=(s, lax.rem(c + k, n_col)), device_id_type=mesh_id
        )
    for k in range(1, n_sample):
        pl.semaphore_signal(
            barrier, inc=1, device_id=(lax.rem(s + k, n_sample), c), device_id_type=mesh_id
        )
    fetch.wait()
    sums_col[c] = jnp.sum(feats_ref[...], axis=0, keepdims=True)
    cols[s, c] = feats_ref[:, col_at(c)]
    rows[s, c] = feats_ref[:, row_at(s)]
    pl.semaphore_wait(barrier, n_col - 1 + n_sample - 1)

    first_cols, first_sums, first_rows = [], [], []
    for k in range(1, n_col):
        to = lax.rem(c + k, n_col)
        first_sums.append(
            send(sums_col.at[c], sums_col.at[c], sum_send.at[k], sum_recv.at[k], s, to)
        )
        first_cols.append(
            send(feats_ref.at[:, col_at(to)], cols.at[s, c], col_send.at[k], col_recv.at[k], s, to)
        )
    for k in range(1, n_sample):
        to = lax.rem(s + k, n_sample)
        first_rows.append(
            send(feats_ref.at[:, row_at(to)], rows.at[s, c], row_send.at[k], row_recv.at[k], to, c)
        )

    pair = 2 if n_sample % 2 == 0 else 1
    n_pairs = n_sample // pair
    mine = lax.rem(s, pair)
    sibling = s + 1 - 2 * mine

    def same_side(k):
        return lax.rem(s // pair + k + n_pairs, n_pairs) * pair + mine

    def hand_on(slot, k):
        return send(cols.at[slot], cols.at[slot], pair_send.at[k], pair_recv.at[k], sibling, c)

    def hop(plane, to, index):
        return pltpu.make_async_remote_copy(
            src_ref=rows.at[:, plane],
            dst_ref=rows.at[:, plane],
            send_sem=rows_send.at[index],
            recv_sem=rows_recv.at[index],
            device_id=(s, to),
            device_id_type=mesh_id,
        )

    def send_right(k):
        return (c + 1 < n_col) & (c >= k - 1)

    def send_left(k):
        return (c >= 1) & (c + k - 1 < n_col)

    def right(k):
        return hop(lax.rem(c - k + 1 + n_col, n_col), lax.rem(c + 1, n_col), k)

    def left(k):
        return hop(lax.rem(c + k - 1, n_col), lax.rem(c - 1 + n_col, n_col), n_col + k)

    def start_hops(k):
        @pl.when(send_right(k))
        def _():
            right(k).start()

        @pl.when(send_left(k))
        def _():
            left(k).start()

    def finish_hops(k):
        @pl.when(c >= k)
        def _():
            right(k).wait_recv()

        @pl.when(c + k < n_col)
        def _():
            left(k).wait_recv()

    for copy in first_sums:
        copy.wait_recv()
    sums_sample[s] = jnp.sum(sums_col[...], axis=0)
    second_sums = []
    for k in range(1, n_sample):
        to = lax.rem(s + k, n_sample)
        second_sums.append(
            send(sums_sample.at[s], sums_sample.at[s], total_send.at[k], total_recv.at[k], to, c)
        )
    for copy in first_rows:
        copy.wait_recv()
    start_hops(1)
    for copy in first_cols:
        copy.wait_recv()
    second_cols = []
    for k in range(1, n_pairs):
        second_cols.append(
            send(cols.at[s], cols.at[s], cols_send.at[k], cols_recv.at[k], same_side(k), c)
        )
    handed = [hand_on(s, 0)] if pair == 2 else []
    for copy in second_sums:
        copy.wait_recv()
    mean_ref[...] = jnp.sum(sums_sample[...], axis=0) * (1.0 / total_images)

    def prepare(slot):
        values = cols[slot].reshape(n_col * images, col_width) - mean_ref[:, col_at(c)]
        high = values.astype(jnp.bfloat16)
        cols_high[slot] = high
        cols_low[slot] = (values - high.astype(jnp.float32)).astype(jnp.bfloat16)

    prepare(s)
    for k in range(1, max(n_col, n_pairs)):
        if k < n_pairs:
            second_cols[k - 1].wait_recv()
            if pair == 2:
                handed.append(hand_on(same_side(-k), k))
        if k < n_col:
            finish_hops(k)
            if k + 1 < n_col:
                start_hops(k + 1)
        if k < n_pairs:
            prepare(same_side(-k))
    for k, copy in enumerate(handed):
        copy.wait_recv()
        prepare(same_side(-k) + 1 - 2 * mine)
    row_values = rows[...].reshape(total_images, row_width) - mean_ref[:, row_at(s)]
    row_values = row_values.T
    row_high = row_values.astype(jnp.bfloat16)
    row_low = (row_values - row_high.astype(jnp.float32)).astype(jnp.bfloat16)
    col_high = cols_high[...].reshape(total_images, col_width)
    col_low = cols_low[...].reshape(total_images, col_width)
    product = jnp.dot(row_high, col_low, preferred_element_type=jnp.float32)
    product += jnp.dot(row_low, col_high, preferred_element_type=jnp.float32)
    product += jnp.dot(row_high, col_high, preferred_element_type=jnp.float32)
    cov_ref[...] = product * (1.0 / (total_images - 1))
    for copy in first_cols + first_sums + first_rows + second_cols + second_sums + handed:
        copy.wait_send()
    for k in range(1, n_col):

        @pl.when(send_right(k))
        def _():
            right(k).wait_send()

        @pl.when(send_left(k))
        def _():
            left(k).wait_send()


def exchange(features):
    n_sample = lax.axis_size("sample")
    n_col = lax.axis_size("col")
    images, width = features.shape
    row_width = width // n_sample
    col_width = width // n_col
    dma = pltpu.SemaphoreType.DMA
    vmem = pl.BlockSpec(memory_space=pltpu.VMEM)
    mean, covariance = pl.pallas_call(
        functools.partial(exchange_kernel, n_sample, n_col),
        out_shape=(
            jax.ShapeDtypeStruct((1, width), jnp.float32),
            jax.ShapeDtypeStruct((row_width, col_width), jnp.float32),
        ),
        in_specs=[pl.BlockSpec(memory_space=pltpu.HBM)],
        out_specs=(vmem, vmem),
        scratch_shapes=[
            pltpu.VMEM((images, width), jnp.float32),
            pltpu.VMEM((n_sample, n_col * images, col_width), jnp.bfloat16),
            pltpu.VMEM((n_sample, n_col * images, col_width), jnp.bfloat16),
            pltpu.VMEM((n_sample, n_col, images, col_width), jnp.float32),
            pltpu.VMEM((n_sample, n_col, images, row_width), jnp.float32),
            pltpu.VMEM((n_col, 1, width), jnp.float32),
            pltpu.VMEM((n_sample, 1, width), jnp.float32),
            dma((n_col,)),
            dma((n_col,)),
            dma((n_sample,)),
            dma((n_sample,)),
            dma((n_col,)),
            dma((n_col,)),
            dma((n_sample,)),
            dma((n_sample,)),
            dma((2 * n_col,)),
            dma((2 * n_col,)),
            dma((n_sample,)),
            dma((n_sample,)),
            dma((n_sample,)),
            dma((n_sample,)),
            dma,
        ],
        compiler_params=pltpu.CompilerParams(
            collective_id=0, has_side_effects=True, vmem_limit_bytes=64 * 1024 * 1024 - 64 * 1024
        ),
        name="exchange",
    )(features)
    return mean.reshape(width), covariance


def local(
    block_inputs,
    first_entry,
    first_wide,
    first_row,
    first_column,
    first_reduce,
    second_entry,
    second_row,
    second_column,
    second_deep,
    deep_row,
    deep_column,
    pool_project,
):
    features = network(
        block_inputs,
        first_entry,
        first_wide,
        first_row,
        first_column,
        first_reduce,
        second_entry,
        second_row,
        second_column,
        second_deep,
        deep_row,
        deep_column,
        pool_project,
    )
    return exchange(features)


def solution(mesh):
    placed = (
        P(("sample", "col"), None, None, None),
        P(),
        P(),
        P(),
        P(),
        P(),
        P(),
        P(),
        P(),
        P(),
        P(),
        P(),
        P(),
    )
    return jax.shard_map(
        local, mesh=mesh, in_specs=placed, out_specs=(P(), P("sample", "col")), check_vma=False
    )
```
